512 devices in a mesh: rows: 32 (over z, core), pairs: 16 (over y, x).
Axes of the slice: x: 4, y: 4, z: 16, core: 2. Of those that a mesh axis runs over, the one named last changes fastest.
Arguments:
- matrix: float32 [4096, 8192], P('rows', 'pairs'), may hold values from -40 to 40
- plan: int32 [2, 64], replicated, may hold values from 0 to 63, as said below
Outputs:
- rotated_matrix: float32 [4096, 8192], P('rows', 'pairs')
The draws below stay inside these ranges and needn't reach their ends.
Inputs may be any that keep to these rules, and one draw needn't show every extreme that they name: Each row plan[r] is a permutation of the 64 slots. Slots 4 j .. 4 j + 3 are those of index j of pairs. From one arrangement to the next at most one block goes from each index j to j + 1 and at most one to j - 1 (none farther and none from the last index to the first or back); all other blocks stay at their index.
All inputs are finite; a program needn't handle non-finite values.
Results may differ from the reference program's by a relative error of at most 0.0003.
Values sent between devices are 32-bit elements; how exact they have to be, the bound alone decides.
A program may use at most 128 MiB of HBM per device.

```python
import math
import jax
import jax.numpy as jnp
import numpy as np
from jax import lax

BLK = 128
ROUNDS = 2
STEPS = 4
ROWS = 4096
NBLK = 64


def draw_matrix(key, part):
    key = jax.random.fold_in(key, 11)
    key_base, key_cols, key_rows = jax.random.split(key, 3)
    col_scale = jnp.exp(jax.random.uniform(key_cols, (1, NBLK * BLK), jnp.float32, math.log(0.3), math.log(3.0)))
    row_scale = jnp.exp(jax.random.uniform(key_rows, (ROWS, 1), jnp.float32, math.log(0.5), math.log(2.0)))
    base = jnp.clip(jax.random.normal(key_base, (ROWS, NBLK * BLK), jnp.float32), -5.0, 5.0)
    return (base * row_scale * col_scale).astype(jnp.float32)


def draw_plan(key, part):
    key = jax.random.fold_in(key, 23)
    pair_total = NBLK // 2
    circle = np.zeros(NBLK, dtype=np.int32)
    for pair_no in range(pair_total):
        if pair_no == 0:
            circle[0] = 0
        elif pair_no == 1:
            circle[2] = 1
        else:
            circle[2 * pair_no] = 2 * (pair_no - 1)
        if pair_no == pair_total - 1:
            circle[2 * pair_no + 1] = 2 * pair_no
        else:
            circle[2 * pair_no + 1] = 2 * (pair_no + 1) + 1
    circle_table = jnp.asarray(circle).reshape(NBLK // 4, 4)
    scores = jax.random.randint(key, (ROUNDS, NBLK // 4, 4), 0, 1 << 20, dtype=jnp.int32)
    scores = scores * 4 + jnp.arange(4, dtype=jnp.int32)[None, None, :]
    shuffles = jnp.argsort(scores, axis=2, stable=True).astype(jnp.int32)
    picked = jnp.take_along_axis(jnp.broadcast_to(circle_table, (ROUNDS, NBLK // 4, 4)), shuffles, axis=2)
    return picked.reshape(ROUNDS, NBLK).astype(jnp.int32)


def setup_inputs(seed: int = 0) -> dict:
    streams_of = jax.random.split(jax.random.key(seed), 3)
    matrix = draw_matrix(jax.random.fold_in(streams_of[2], 71), 0)
    plan = draw_plan(jax.random.fold_in(streams_of[2], 71), 0)
    return {"matrix": matrix, "plan": plan}


def tournament(full_width, steps_count):
    half_cols = full_width // 2

    def place(position):
        return position if position < half_cols else full_width - 1 - position + half_cols

    def before(position):
        if position == 0:
            return 0
        if position == 1:
            return full_width - 1
        return position - 1
    start = np.zeros(full_width, dtype=np.int32)
    moves = np.zeros(full_width, dtype=np.int32)
    for position in range(full_width):
        start[place(position)] = position
        moves[place(position)] = place(before(position))
    layout = start.copy()
    for step_no in range(steps_count):
        layout = layout[moves]
    undo = np.argsort(layout).astype(np.int32)
    return (start, moves, undo)

def take_static(array_in, index_list, axis_no):
    pieces = []
    first = 0
    total = len(index_list)
    while first < total:
        last = first
        while last + 1 < total and int(index_list[last + 1]) == int(index_list[last]) + 1:
            last = last + 1
        begin = int(index_list[first])
        pieces.append(lax.slice_in_dim(array_in, begin, begin + last - first + 1, axis=axis_no))
        first = last + 1
    if len(pieces) == 1:
        return pieces[0]
    return jnp.concatenate(pieces, axis=axis_no)

def jacobi_tangent(upper_a, lower_b, coupling):
    differ = lower_b - upper_a
    sign_val = jnp.where(differ >= 0.0, 1.0, -1.0)
    denom = jnp.abs(differ) + jnp.sqrt(differ * differ + 4.0 * coupling * coupling)
    positive = denom > 0.0
    safe_den = jnp.where(positive, denom, 1.0)
    return jnp.where(positive, 2.0 * coupling * sign_val / safe_den, 0.0)

def rotate_gram(gram_mat, steps_count):
    full_width = gram_mat.shape[-1]
    half_cols = full_width // 2
    start, moves, undo = tournament(full_width, steps_count)
    current = take_static(take_static(gram_mat, start, 1), start, 2)
    vectors = jnp.broadcast_to(jnp.asarray(np.eye(full_width, dtype=np.float32)[:, start]), gram_mat.shape)
    for step_no in range(steps_count):
        upper_a = jnp.diagonal(current[:, :half_cols, :half_cols], axis1=1, axis2=2)
        lower_b = jnp.diagonal(current[:, half_cols:, half_cols:], axis1=1, axis2=2)
        coupling = jnp.diagonal(current[:, :half_cols, half_cols:], axis1=1, axis2=2)
        tangent = jacobi_tangent(upper_a, lower_b, coupling)
        cosine = 1.0 / jnp.sqrt(1.0 + tangent * tangent)
        sine_val = cosine * tangent
        col_cos = cosine[:, None, :]
        col_sin = sine_val[:, None, :]
        left_part = current[:, :, :half_cols]
        right_part = current[:, :, half_cols:]
        current = jnp.concatenate([left_part * col_cos - right_part * col_sin, left_part * col_sin + right_part * col_cos], axis=2)
        row_cos = cosine[:, :, None]
        row_sin = sine_val[:, :, None]
        top_part = current[:, :half_cols, :]
        bottom_part = current[:, half_cols:, :]
        current = jnp.concatenate([top_part * row_cos - bottom_part * row_sin, top_part * row_sin + bottom_part * row_cos], axis=1)
        left_vec = vectors[:, :, :half_cols]
        right_vec = vectors[:, :, half_cols:]
        vectors = jnp.concatenate([left_vec * col_cos - right_vec * col_sin, left_vec * col_sin + right_vec * col_cos], axis=2)
        current = take_static(take_static(current, moves, 1), moves, 2)
        vectors = take_static(vectors, moves, 2)
    return take_static(vectors, undo, 2)

def reference(matrix, plan):
    rows_all = matrix.shape[0]
    current = matrix
    for round_no in range(ROUNDS):
        blocks = current.reshape(rows_all, NBLK, BLK)[:, plan[round_no]]
        paired = blocks.reshape(rows_all, NBLK // 2, 2 * BLK)
        gram_mat = jnp.einsum('rpi,rpj->pij', paired, paired, precision=lax.Precision.HIGHEST)
        rotation = rotate_gram(gram_mat, STEPS)
        paired = jnp.einsum('rpi,pij->rpj', paired, rotation, precision=lax.Precision.HIGHEST)
        current = paired.reshape(rows_all, NBLK * BLK)
    return current
```

```python
import functools

import jax
import jax.numpy as jnp
from jax import lax
from jax.experimental import pallas as pl
from jax.experimental.pallas import tpu as pltpu
from jax.sharding import PartitionSpec as P

MESH = pl.DeviceIdType.MESH
BLK = 128
ROUNDS = 2
STEPS = 4
SLOTS = 4
GROUP = 4
LANES = 128
F32 = jnp.float32
HOPS = ((2, 0), (2, 1), (3, 0), (3, 1), (1, 0), (1, 1), (0, 1))


def roll(x, by):
    return pltpu.roll(x, by % x.shape[1], 1)


def lane_of(shape):
    return lax.broadcasted_iota(jnp.int32, shape, 1)


def pick(x, index):
    return jnp.take_along_axis(x, index, axis=1)


def extra_lanes(slot):
    first = jnp.where(slot < 3, 0, jnp.where(slot < 5, 1, 2))
    second = jnp.where(slot < 3, 2 * slot + 1, jnp.where(slot == 3, 2, jnp.where(slot == 4, 4, 3)))
    return first, jnp.minimum(second, 7)


def band_terms(left, right, reverse):
    lane = lane_of(left.shape)
    top, bottom = left, pick(right, reverse)
    back = pick(left, reverse)
    tops = [top] + [roll(jnp.where(lane < d, right, top), -d) for d in (2, 4, 6)]
    bottoms = [bottom] + [roll(jnp.where(lane < d, back, bottom), -d) for d in (2, 4, 6)]
    first, second = extra_lanes(lane % 8)
    one = jnp.where(lane < 16, pick(top, first), pick(bottom, first))
    two = jnp.where(lane % 16 < 8, pick(top, second), pick(bottom, second))
    terms = [top * t for t in tops] + [top * b for b in bottoms]
    terms += [one * two] + [bottom * t for t in tops[1:]] + [bottom * b for b in bottoms]
    return top, bottom, terms


def tangent_of(upper_a, lower_b, coupling):
    differ = lower_b - upper_a
    sign_val = jnp.where(differ >= 0.0, 1.0, -1.0)
    denom = jnp.abs(differ) + jnp.sqrt(differ * differ + 4.0 * coupling * coupling)
    positive = denom > 0.0
    safe_den = jnp.where(positive, denom, 1.0)
    return jnp.where(positive, 2.0 * coupling * sign_val / safe_den, 0.0)


def rotate_both(top, bottom, cosine, sine):
    return top * cosine - bottom * sine, top * sine + bottom * cosine


def angles(tt, tb, bt, bb):
    shape = tt.shape
    lane = lane_of(shape)
    row = lax.broadcasted_iota(jnp.int32, shape, 0)
    first, second = extra_lanes(jnp.minimum(lane, 5))
    ahead = lane + 2 * row
    over = ahead > LANES - 1
    is_extra = row == 4
    at_i = jnp.where(is_extra, first, lane)
    at_j = jnp.where(is_extra, second, jnp.where(row > 4, lane, jnp.where(over, 2 * LANES - 1 - ahead, ahead)))
    flip = jnp.where(over & (row < 4), -1.0, 1.0)

    def line(x, r):
        return jnp.broadcast_to(x[r : r + 1], shape)

    def item(x, r, i):
        return jnp.broadcast_to(x[r : r + 1, i : i + 1], shape)

    def up(x):
        return pltpu.roll(x, shape[0] - 1, 0)

    def down(x):
        return pltpu.roll(x, 1, 0)

    cosines, sines = [], []
    for step_no in range(STEPS):
        tangent = tangent_of(line(tt, 0), line(bb, 0), line(tb, 0))
        cosine = 1.0 / jnp.sqrt(1.0 + tangent * tangent)
        sine = cosine * tangent
        cosines.append(cosine[0:1])
        sines.append(sine[0:1])
        if step_no == STEPS - 1:
            break
        cos_i, sin_i = pick(cosine, at_i), pick(sine, at_i)
        cos_j, sin_j = pick(cosine, at_j), pick(sine, at_j) * flip
        tt, tb = rotate_both(tt, tb, cos_j, sin_j)
        bt, bb = rotate_both(bt, bb, cos_j, sin_j)
        tt, bt = rotate_both(tt, bt, cos_i, sin_i)
        tb, bb = rotate_both(tb, bb, cos_i, sin_i)
        new_tt = jnp.where(
            lane >= 2,
            roll(tt, 1),
            jnp.where(
                lane == 1,
                jnp.where(row == 0, roll(bb, 1), roll(bt, 1)),
                jnp.where(row == 0, tt, pick(line(tt, 4), jnp.maximum(row - 1, 0))),
            ),
        )
        new_bb = jnp.where(lane < LANES - 1, roll(bb, -1), pick(tt, LANES - 1 - 2 * row))
        new_tb = jnp.where(
            lane >= 2,
            roll(up(tb), 1),
            jnp.where(lane == 1, roll(up(bb), 1), pick(line(tb, 4), row)),
        )
        new_bt = jnp.where(
            row == 0,
            new_tb,
            jnp.where(
                lane < LANES - 1,
                roll(down(bt), -1),
                pick(down(bt), jnp.minimum(LANES + 1 - 2 * row, LANES - 1)),
            ),
        )
        head = lane == 0
        second_one = lane == 1
        extra_tt = jnp.where(head, item(tb, 0, 0), jnp.where(second_one, item(tt, 1, 0), item(bt, 4, 0)))
        extra_tb = jnp.where(head, item(tb, 1, 0), jnp.where(second_one, item(tb, 2, 0), item(bb, 4, 1)))
        extra_bt = jnp.where(head, item(bb, 4, 0), jnp.where(second_one, item(bt, 4, 3), item(tb, 4, 3)))
        extra_bb = jnp.where(head, item(bb, 4, 3), jnp.where(second_one, item(bb, 4, 4), item(bb, 4, 5)))
        tt = jnp.where(is_extra, extra_tt, new_tt)
        tb = jnp.where(is_extra, extra_tb, new_tb)
        bt = jnp.where(is_extra, extra_bt, new_bt)
        bb = jnp.where(is_extra, extra_bb, new_bb)
    return cosines, sines


def apply_steps(top, bottom, cosines, sines):
    lane = lane_of(top.shape)
    for step_no in range(STEPS):
        top, bottom = rotate_both(top, bottom, cosines[step_no], sines[step_no])
        if step_no < STEPS - 1:
            new_top = jnp.where(lane == 0, top, roll(jnp.where(lane == 0, bottom, top), 1))
            bottom = jnp.where(lane == LANES - 1, top, roll(bottom, -1))
            top = new_top
    last = STEPS - 1
    turn = 2 * LANES - 1 - last
    keep = LANES - last
    left = jnp.where(
        lane == 0,
        top,
        jnp.where(lane < keep, roll(top, -last), pick(bottom, jnp.minimum(turn - lane, LANES - 1))),
    )
    right = jnp.where(
        lane < keep, pick(bottom, jnp.maximum(turn - LANES - lane, 0)), roll(top, LANES - 1 - last)
    )
    return left, right


def kernel(
    n_rows, n_pairs, plan_ref, x_ref, o_ref,
    first, second, came, sent, sides, result, bands, parts, sums, entries, turns,
    in_sem, out_sem, block_out, block_in, part_out, part_in, sum_out, sum_in, turn_out, turn_in,
):
    rows_at = lax.axis_index("rows")
    index = lax.axis_index("pairs")
    z, core = rows_at // 2, rows_at % 2
    n_chips = n_rows // 2
    group, member = z // GROUP, z % GROUP
    local_rows = x_ref.shape[0]

    def device(chip, which_core):
        return (chip * 2 + which_core, index)

    def in_group(step):
        return group * GROUP + (member + step) % GROUP

    ahead = (rows_at, (index + 1) % n_pairs)
    behind = (rows_at, (index + n_pairs - 1) % n_pairs)
    across = jnp.where(member < 2, z + n_chips // 2 + 2, z + n_chips // 2 - 2) % n_chips
    far = (
        across,
        (z + GROUP) % n_chips,
        (z + n_chips - GROUP) % n_chips,
    )
    near = [device(in_group(step), (core + turn) % 2) for step, turn in HOPS]
    peers = [ahead, behind] + near + [device(chip, core) for chip in far]

    barrier = pltpu.get_barrier_semaphore()
    for peer in peers:
        pl.semaphore_signal(barrier, inc=1, device_id=peer, device_id_type=MESH)
    loads = [
        pltpu.make_async_copy(
            x_ref.at[:, pl.ds(s * BLK, BLK)], first.at[s], in_sem.at[s]
        )
        for s in range(SLOTS)
    ]
    for load in loads:
        load.start()
    for load in loads:
        load.wait()

    def remote(src, dst, send_sem, recv_sem, to):
        return pltpu.make_async_remote_copy(
            src_ref=src, dst_ref=dst, send_sem=send_sem, recv_sem=recv_sem,
            device_id=to, device_id_type=MESH,
        )

    chunk = 8
    steps = local_rows // chunk
    shape = (chunk, LANES)
    reverse = LANES - 1 - lane_of(shape)
    started = []
    pl.semaphore_wait(barrier, len(peers))

    for rnd in range(ROUNDS):
        held = (first, second)[rnd]
        to_ahead = jnp.int32(0)
        to_behind = jnp.int32(0)
        for s in range(SLOTS):
            took = plan_ref[rnd, ahead[1] * SLOTS + s] - index * SLOTS
            to_ahead = jnp.where((took >= 0) & (took < SLOTS), took, to_ahead)
            took = plan_ref[rnd, behind[1] * SLOTS + s] - index * SLOTS
            to_behind = jnp.where((took >= 0) & (took < SLOTS), took, to_behind)
        sent[rnd, 0] = held[to_ahead]
        sent[rnd, 1] = held[to_behind]
        moves = [
            remote(sent.at[rnd, 0], came.at[rnd, 0], block_out.at[rnd, 0], block_in.at[rnd, 0], ahead),
            remote(sent.at[rnd, 1], came.at[rnd, 1], block_out.at[rnd, 1], block_in.at[rnd, 1], behind),
        ]
        for move in moves:
            move.start()
        for move in moves:
            move.wait_recv()
        started += moves

        for pair in range(2):
            at = []
            for side in range(2):
                took = plan_ref[rnd, index * SLOTS + 2 * pair + side] - index * SLOTS
                at.append(took)

            def add_rows(i, acc, pair=pair, at=at, rnd=rnd, held=held):
                rows = pl.ds(pl.multiple_of(i * chunk, chunk), chunk)
                blocks = [
                    jnp.where(
                        took < 0,
                        came[rnd, 0, rows, :],
                        jnp.where(took >= SLOTS, came[rnd, 1, rows, :], held[jnp.clip(took, 0, SLOTS - 1), rows, :]),
                    )
                    for took in at
                ]
                top, bottom, terms = band_terms(*blocks, reverse)
                sides[pair, 0, rows, :] = top
                sides[pair, 1, rows, :] = bottom
                return tuple(a + t for a, t in zip(acc, terms))

            acc = lax.fori_loop(0, steps, add_rows, (jnp.zeros(shape, F32),) * 16)
            for k in range(16):
                bands[rnd, pair, k : k + 1] = jnp.sum(acc[k], axis=0, keepdims=True)

        for k, (step, turn) in enumerate(HOPS):
            there = (core + turn) % 2
            copy = remote(
                bands.at[rnd, there], parts.at[rnd, member * 2 + core],
                part_out.at[rnd, k], part_in.at[rnd, k], device(in_group(step), there),
            )
            copy.start()
            started.append(copy)
        parts[rnd, member * 2 + core] = bands[rnd, core]
        for k, (step, turn) in enumerate(HOPS):
            source = (in_group(GROUP - step) % GROUP) * 2 + (core + turn) % 2
            remote(
                bands.at[rnd, core], parts.at[rnd, source],
                part_out.at[rnd, k], part_in.at[rnd, k], device(in_group(GROUP - step), (core + turn) % 2),
            ).wait_recv()
        total = parts[rnd, 0]
        for k in range(1, 2 * GROUP):
            total = total + parts[rnd, k]
        sums[rnd, group] = total

        for k, chip in enumerate(far):
            copy = remote(
                sums.at[rnd, group], sums.at[rnd, group],
                sum_out.at[rnd, k], sum_in.at[rnd, k], device(chip, core),
            )
            copy.start()
            started.append(copy)
        for k, chip in enumerate((far[0], far[2], far[1])):
            remote(
                sums.at[rnd, group], sums.at[rnd, chip // GROUP],
                sum_out.at[rnd, k], sum_in.at[rnd, k], device(chip, core),
            ).wait_recv()
        total = sums[rnd, 0]
        for k in range(1, n_chips // GROUP):
            total = total + sums[rnd, k]

        entries[...] = jnp.zeros(entries.shape, F32)
        for k in range(4):
            entries[k, 0:4] = total[4 * k : 4 * k + 4]
        entries[2, 0:1] = total[4:5]
        for k in range(4):
            entries[k, 4:5] = roll(jnp.broadcast_to(total[8:9], shape), -8 * k)[0:1]
        cosines, sines = angles(entries[0], entries[1], entries[2], entries[3])
        for k in range(STEPS):
            turns[rnd, core, k : k + 1] = cosines[k]
            turns[rnd, core, STEPS + k : STEPS + k + 1] = sines[k]
        other = device(z, 1 - core)
        copy = remote(turns.at[rnd, core], turns.at[rnd, core], turn_out.at[rnd], turn_in.at[rnd], other)
        copy.start()
        started.append(copy)
        remote(
            turns.at[rnd, core], turns.at[rnd, 1 - core], turn_out.at[rnd], turn_in.at[rnd], other
        ).wait_recv()

        for pair in range(2):
            lines = [jnp.broadcast_to(turns[rnd, pair, k : k + 1], shape) for k in range(2 * STEPS)]

            def turn_rows(i, carry, pair=pair, lines=lines, rnd=rnd):
                rows = pl.ds(pl.multiple_of(i * chunk, chunk), chunk)
                left, right = apply_steps(
                    sides[pair, 0, rows, :], sides[pair, 1, rows, :], lines[:STEPS], lines[STEPS:]
                )
                if rnd < ROUNDS - 1:
                    second[2 * pair, rows, :] = left
                    second[2 * pair + 1, rows, :] = right
                else:
                    result[2 * pair, rows, :] = left
                    result[2 * pair + 1, rows, :] = right
                return carry

            lax.fori_loop(0, steps, turn_rows, 0)

    stores = [
        pltpu.make_async_copy(result.at[s], o_ref.at[:, pl.ds(s * BLK, BLK)], out_sem.at[s])
        for s in range(SLOTS)
    ]
    for store in stores:
        store.start()
    for copy in started:
        copy.wait_send()
    for store in stores:
        store.wait()


def on_device(n_rows, n_pairs, matrix, plan):
    rows, cols = matrix.shape
    dma = pltpu.SemaphoreType.DMA
    near, far = len(HOPS), n_rows // 2 // GROUP - 1
    return pl.pallas_call(
        functools.partial(kernel, n_rows, n_pairs),
        out_shape=jax.ShapeDtypeStruct((rows, cols), F32),
        in_specs=[
            pl.BlockSpec(memory_space=pltpu.SMEM),
            pl.BlockSpec(memory_space=pl.ANY),
        ],
        out_specs=pl.BlockSpec(memory_space=pl.ANY),
        scratch_shapes=[
            pltpu.VMEM((SLOTS, rows, BLK), F32),
            pltpu.VMEM((SLOTS, rows, BLK), F32),
            pltpu.VMEM((ROUNDS, 2, rows, BLK), F32),
            pltpu.VMEM((ROUNDS, 2, rows, BLK), F32),
            pltpu.VMEM((2, 2, rows, BLK), F32),
            pltpu.VMEM((SLOTS, rows, BLK), F32),
            pltpu.VMEM((ROUNDS, 2, 16, BLK), F32),
            pltpu.VMEM((ROUNDS, 2 * GROUP, 16, BLK), F32),
            pltpu.VMEM((ROUNDS, far + 1, 16, BLK), F32),
            pltpu.VMEM((4, 8, BLK), F32),
            pltpu.VMEM((ROUNDS, 2, 2 * STEPS, BLK), F32),
            dma((SLOTS,)),
            dma((SLOTS,)),
            dma((ROUNDS, 2)),
            dma((ROUNDS, 2)),
            dma((ROUNDS, near)),
            dma((ROUNDS, near)),
            dma((ROUNDS, far)),
            dma((ROUNDS, far)),
            dma((ROUNDS,)),
            dma((ROUNDS,)),
        ],
        compiler_params=pltpu.CompilerParams(
            collective_id=0, has_side_effects=True, vmem_limit_bytes=32 * 1024 * 1024
        ),
    )(plan, matrix)


def solution(mesh):
    return jax.shard_map(
        functools.partial(on_device, mesh.shape["rows"], mesh.shape["pairs"]),
        mesh=mesh,
        in_specs=(P("rows", "pairs"), P()),
        out_specs=P("rows", "pairs"),
        check_vma=False,
    )
```

```python
import functools

import jax
import jax.numpy as jnp
from jax import lax
from jax.experimental import pallas as pl
from jax.experimental.pallas import tpu as pltpu
from jax.sharding import PartitionSpec as P

MESH = pl.DeviceIdType.MESH
BLK = 128
ROUNDS = 2
STEPS = 4
SLOTS = 4
GROUP = 4
LANES = 128
F32 = jnp.float32
HOPS = ((2, 0), (2, 1), (3, 0), (3, 1), (1, 0), (1, 1), (0, 1))


def roll(x, by):
    return pltpu.roll(x, by % x.shape[1], 1)


def lane_of(shape):
    return lax.broadcasted_iota(jnp.int32, shape, 1)


def pick(x, index):
    return jnp.take_along_axis(x, index, axis=1)


def extra_lanes(slot):
    first = jnp.where(slot < 3, 0, jnp.where(slot < 5, 1, 2))
    second = jnp.where(slot < 3, 2 * slot + 1, jnp.where(slot == 3, 2, jnp.where(slot == 4, 4, 3)))
    return first, jnp.minimum(second, 7)


def band_terms(left, right, reverse):
    lane = lane_of(left.shape)
    top, bottom = left, pick(right, reverse)
    back = pick(left, reverse)
    tops = [top] + [roll(jnp.where(lane < d, right, top), -d) for d in (2, 4, 6)]
    bottoms = [bottom] + [roll(jnp.where(lane < d, back, bottom), -d) for d in (2, 4, 6)]
    first, second = extra_lanes(lane % 8)
    one = jnp.where(lane < 16, pick(top, first), pick(bottom, first))
    two = jnp.where(lane % 16 < 8, pick(top, second), pick(bottom, second))
    terms = [top * t for t in tops] + [top * b for b in bottoms]
    terms += [one * two] + [bottom * t for t in tops[1:]] + [bottom * b for b in bottoms]
    return top, bottom, terms


def fold(x):
    total = x[0:8]
    for first in range(8, x.shape[0], 8):
        total = total + x[first : first + 8]
    return total


def tangent_of(upper_a, lower_b, coupling):
    differ = lower_b - upper_a
    sign_val = jnp.where(differ >= 0.0, 1.0, -1.0)
    denom = jnp.abs(differ) + jnp.sqrt(differ * differ + 4.0 * coupling * coupling)
    positive = denom > 0.0
    safe_den = jnp.where(positive, denom, 1.0)
    return jnp.where(positive, 2.0 * coupling * sign_val / safe_den, 0.0)


def rotate_both(top, bottom, cosine, sine):
    return top * cosine - bottom * sine, top * sine + bottom * cosine


def angles(tt, tb, bt, bb):
    shape = tt.shape
    lane = lane_of(shape)
    row = lax.broadcasted_iota(jnp.int32, shape, 0)
    first, second = extra_lanes(jnp.minimum(lane, 5))
    ahead = lane + 2 * row
    over = ahead > LANES - 1
    is_extra = row == 4
    at_i = jnp.where(is_extra, first, lane)
    at_j = jnp.where(is_extra, second, jnp.where(row > 4, lane, jnp.where(over, 2 * LANES - 1 - ahead, ahead)))
    flip = jnp.where(over & (row < 4), -1.0, 1.0)

    def line(x, r):
        return jnp.broadcast_to(x[r : r + 1], shape)

    def item(x, r, i):
        return jnp.broadcast_to(x[r : r + 1, i : i + 1], shape)

    def up(x):
        return pltpu.roll(x, shape[0] - 1, 0)

    def down(x):
        return pltpu.roll(x, 1, 0)

    cosines, sines = [], []
    for step_no in range(STEPS):
        tangent = tangent_of(line(tt, 0), line(bb, 0), line(tb, 0))
        cosine = 1.0 / jnp.sqrt(1.0 + tangent * tangent)
        sine = cosine * tangent
        cosines.append(cosine[0:1])
        sines.append(sine[0:1])
        if step_no == STEPS - 1:
            break
        cos_i, sin_i = pick(cosine, at_i), pick(sine, at_i)
        cos_j, sin_j = pick(cosine, at_j), pick(sine, at_j) * flip
        tt, tb = rotate_both(tt, tb, cos_j, sin_j)
        bt, bb = rotate_both(bt, bb, cos_j, sin_j)
        tt, bt = rotate_both(tt, bt, cos_i, sin_i)
        tb, bb = rotate_both(tb, bb, cos_i, sin_i)
        new_tt = jnp.where(
            lane >= 2,
            roll(tt, 1),
            jnp.where(
                lane == 1,
                jnp.where(row == 0, roll(bb, 1), roll(bt, 1)),
                jnp.where(row == 0, tt, pick(line(tt, 4), jnp.maximum(row - 1, 0))),
            ),
        )
        new_bb = jnp.where(lane < LANES - 1, roll(bb, -1), pick(tt, LANES - 1 - 2 * row))
        new_tb = jnp.where(
            lane >= 2,
            roll(up(tb), 1),
            jnp.where(lane == 1, roll(up(bb), 1), pick(line(tb, 4), row)),
        )
        new_bt = jnp.where(
            row == 0,
            new_tb,
            jnp.where(
                lane < LANES - 1,
                roll(down(bt), -1),
                pick(down(bt), jnp.minimum(LANES + 1 - 2 * row, LANES - 1)),
            ),
        )
        head = lane == 0
        second_one = lane == 1
        extra_tt = jnp.where(head, item(tb, 0, 0), jnp.where(second_one, item(tt, 1, 0), item(bt, 4, 0)))
        extra_tb = jnp.where(head, item(tb, 1, 0), jnp.where(second_one, item(tb, 2, 0), item(bb, 4, 1)))
        extra_bt = jnp.where(head, item(bb, 4, 0), jnp.where(second_one, item(bt, 4, 3), item(tb, 4, 3)))
        extra_bb = jnp.where(head, item(bb, 4, 3), jnp.where(second_one, item(bb, 4, 4), item(bb, 4, 5)))
        tt = jnp.where(is_extra, extra_tt, new_tt)
        tb = jnp.where(is_extra, extra_tb, new_tb)
        bt = jnp.where(is_extra, extra_bt, new_bt)
        bb = jnp.where(is_extra, extra_bb, new_bb)
    return cosines, sines


def apply_steps(top, bottom, cosines, sines):
    lane = lane_of(top.shape)
    for step_no in range(STEPS):
        top, bottom = rotate_both(top, bottom, cosines[step_no], sines[step_no])
        if step_no < STEPS - 1:
            new_top = jnp.where(lane == 0, top, roll(jnp.where(lane == 0, bottom, top), 1))
            bottom = jnp.where(lane == LANES - 1, top, roll(bottom, -1))
            top = new_top
    last = STEPS - 1
    turn = 2 * LANES - 1 - last
    keep = LANES - last
    left = jnp.where(
        lane == 0,
        top,
        jnp.where(lane < keep, roll(top, -last), pick(bottom, jnp.minimum(turn - lane, LANES - 1))),
    )
    right = jnp.where(
        lane < keep, pick(bottom, jnp.maximum(turn - LANES - lane, 0)), roll(top, LANES - 1 - last)
    )
    return left, right


def kernel(
    n_rows, n_pairs, plan_in, x_ref, o_ref,
    first, second, came, sent, sides, result, bands, parts, sums, entries, turns, plan_ref,
    plan_sem, ready_sem, in_sem, out_sem, block_out, block_in, part_out, part_in, sum_out, sum_in, turn_out, turn_in,
):
    rows_at = lax.axis_index("rows")
    index = lax.axis_index("pairs")
    z, core = rows_at // 2, rows_at % 2
    n_chips = n_rows // 2
    group, member = z // GROUP, z % GROUP
    local_rows = x_ref.shape[0]

    def device(chip, which_core):
        return (chip * 2 + which_core, index)

    def in_group(step):
        return group * GROUP + (member + step) % GROUP

    ahead = (rows_at, (index + 1) % n_pairs)
    behind = (rows_at, (index + n_pairs - 1) % n_pairs)
    across = jnp.where(member < 2, z + n_chips // 2 + 2, z + n_chips // 2 - 2) % n_chips
    far = (
        across,
        (z + GROUP) % n_chips,
        (z + n_chips - GROUP) % n_chips,
    )
    near = [device(in_group(step), (core + turn) % 2) for step, turn in HOPS]
    line = [device((z + step + n_chips) % n_chips, core) for step in (1, -1, 2, -2, 3, -3)]
    siblings = [device(z, 1 - core)] + [device(in_group(step), 1 - core) for step in (1, 2, 3)]
    peers = line + siblings + [ahead, behind]

    barrier = pltpu.get_barrier_semaphore()
    for peer in peers:
        pl.semaphore_signal(barrier, inc=1, device_id=peer, device_id_type=MESH)
    loads = [pltpu.make_async_copy(plan_in, plan_ref, plan_sem)] + [
        pltpu.make_async_copy(
            x_ref.at[:, pl.ds(s * BLK, BLK)], first.at[s], in_sem.at[s]
        )
        for s in range(SLOTS)
    ]
    for load in loads:
        load.start()
    for load in loads:
        load.wait()

    def remote(src, dst, send_sem, recv_sem, to):
        return pltpu.make_async_remote_copy(
            src_ref=src, dst_ref=dst, send_sem=send_sem, recv_sem=recv_sem,
            device_id=to, device_id_type=MESH,
        )

    shape = (8, LANES)
    gram_rows, turn_chunk = 128, 128
    reverse = LANES - 1 - lane_of((gram_rows, LANES))
    started = []
    pl.semaphore_wait(barrier, len(peers))
    for peer in line[2:]:
        pl.semaphore_signal(ready_sem, inc=1, device_id=peer, device_id_type=MESH)

    for rnd in range(ROUNDS):
        held = (first, second)[rnd]
        to_ahead = jnp.int32(0)
        to_behind = jnp.int32(0)
        for s in range(SLOTS):
            took = plan_ref[rnd, ahead[1] * SLOTS + s] - index * SLOTS
            to_ahead = jnp.where((took >= 0) & (took < SLOTS), took, to_ahead)
            took = plan_ref[rnd, behind[1] * SLOTS + s] - index * SLOTS
            to_behind = jnp.where((took >= 0) & (took < SLOTS), took, to_behind)
        sent[rnd, 0] = held[to_ahead]
        sent[rnd, 1] = held[to_behind]
        moves = [
            remote(sent.at[rnd, 0], came.at[rnd, 0], block_out.at[rnd, 0], block_in.at[rnd, 0], ahead),
            remote(sent.at[rnd, 1], came.at[rnd, 1], block_out.at[rnd, 1], block_in.at[rnd, 1], behind),
        ]
        for move in moves:
            move.start()
        for move in moves:
            move.wait_recv()
        started += moves

        for pair in range(2):
            at = []
            for side in range(2):
                took = plan_ref[rnd, index * SLOTS + 2 * pair + side] - index * SLOTS
                at.append(took)

            def add_rows(i, acc, pair=pair, at=at, rnd=rnd, held=held):
                rows = pl.ds(pl.multiple_of(i * gram_rows, gram_rows), gram_rows)
                blocks = [
                    jnp.where(
                        took < 0,
                        came[rnd, 0, rows, :],
                        jnp.where(took >= SLOTS, came[rnd, 1, rows, :], held[jnp.clip(took, 0, SLOTS - 1), rows, :]),
                    )
                    for took in at
                ]
                top, bottom, terms = band_terms(*blocks, reverse)
                sides[pair, 0, rows, :] = top
                sides[pair, 1, rows, :] = bottom
                return tuple(a + fold(t) for a, t in zip(acc, terms))

            acc = lax.fori_loop(0, local_rows // gram_rows, add_rows, (jnp.zeros(shape, F32),) * 16)
            for k in range(16):
                bands[rnd, pair, k : k + 1] = jnp.sum(acc[k], axis=0, keepdims=True)

        for k, (step, turn) in enumerate(HOPS):
            there = (core + turn) % 2
            copy = remote(
                bands.at[rnd, there], parts.at[rnd, member * 2 + core],
                part_out.at[rnd, k], part_in.at[rnd, k], device(in_group(step), there),
            )
            copy.start()
            started.append(copy)
        parts[rnd, member * 2 + core] = bands[rnd, core]
        for k, (step, turn) in enumerate(HOPS):
            source = (in_group(GROUP - step) % GROUP) * 2 + (core + turn) % 2
            remote(
                bands.at[rnd, core], parts.at[rnd, source],
                part_out.at[rnd, k], part_in.at[rnd, k], device(in_group(GROUP - step), (core + turn) % 2),
            ).wait_recv()
        total = parts[rnd, 0]
        for k in range(1, 2 * GROUP):
            total = total + parts[rnd, k]
        sums[rnd, group] = total

        if rnd == 0:
            pl.semaphore_wait(ready_sem, len(line[2:]))
        for k, chip in enumerate(far):
            copy = remote(
                sums.at[rnd, group], sums.at[rnd, group],
                sum_out.at[rnd, k], sum_in.at[rnd, k], device(chip, core),
            )
            copy.start()
            started.append(copy)
        for k, chip in enumerate((far[0], far[2], far[1])):
            remote(
                sums.at[rnd, group], sums.at[rnd, chip // GROUP],
                sum_out.at[rnd, k], sum_in.at[rnd, k], device(chip, core),
            ).wait_recv()
        total = sums[rnd, 0]
        for k in range(1, n_chips // GROUP):
            total = total + sums[rnd, k]

        entries[...] = jnp.zeros(entries.shape, F32)
        for k in range(4):
            entries[k, 0:4] = total[4 * k : 4 * k + 4]
        entries[2, 0:1] = total[4:5]
        for k in range(4):
            entries[k, 4:5] = roll(jnp.broadcast_to(total[8:9], shape), -8 * k)[0:1]
        cosines, sines = angles(entries[0], entries[1], entries[2], entries[3])
        for k in range(STEPS):
            turns[rnd, core, k : k + 1] = cosines[k]
            turns[rnd, core, STEPS + k : STEPS + k + 1] = sines[k]
        other = device(z, 1 - core)
        copy = remote(turns.at[rnd, core], turns.at[rnd, core], turn_out.at[rnd], turn_in.at[rnd], other)
        copy.start()
        started.append(copy)
        remote(
            turns.at[rnd, core], turns.at[rnd, 1 - core], turn_out.at[rnd], turn_in.at[rnd], other
        ).wait_recv()

        for pair in range(2):
            lines = [jnp.broadcast_to(turns[rnd, pair, k : k + 1], (turn_chunk, LANES)) for k in range(2 * STEPS)]

            def turn_rows(i, carry, pair=pair, lines=lines, rnd=rnd):
                rows = pl.ds(pl.multiple_of(i * turn_chunk, turn_chunk), turn_chunk)
                left, right = apply_steps(
                    sides[pair, 0, rows, :], sides[pair, 1, rows, :], lines[:STEPS], lines[STEPS:]
                )
                if rnd < ROUNDS - 1:
                    second[2 * pair, rows, :] = left
                    second[2 * pair + 1, rows, :] = right
                else:
                    result[2 * pair, rows, :] = left
                    result[2 * pair + 1, rows, :] = right
                return carry

            lax.fori_loop(0, local_rows // turn_chunk, turn_rows, 0)

    stores = [
        pltpu.make_async_copy(result.at[s], o_ref.at[:, pl.ds(s * BLK, BLK)], out_sem.at[s])
        for s in range(SLOTS)
    ]
    for store in stores:
        store.start()
    for copy in started:
        copy.wait_send()
    for store in stores:
        store.wait()


def on_device(n_rows, n_pairs, matrix, plan):
    rows, cols = matrix.shape
    dma = pltpu.SemaphoreType.DMA
    near, far = len(HOPS), n_rows // 2 // GROUP - 1
    return pl.pallas_call(
        functools.partial(kernel, n_rows, n_pairs),
        out_shape=jax.ShapeDtypeStruct((rows, cols), F32),
        in_specs=[
            pl.BlockSpec(memory_space=pl.ANY),
            pl.BlockSpec(memory_space=pl.ANY),
        ],
        out_specs=pl.BlockSpec(memory_space=pl.ANY),
        scratch_shapes=[
            pltpu.VMEM((SLOTS, rows, BLK), F32),
            pltpu.VMEM((SLOTS, rows, BLK), F32),
            pltpu.VMEM((ROUNDS, 2, rows, BLK), F32),
            pltpu.VMEM((ROUNDS, 2, rows, BLK), F32),
            pltpu.VMEM((2, 2, rows, BLK), F32),
            pltpu.VMEM((SLOTS, rows, BLK), F32),
            pltpu.VMEM((ROUNDS, 2, 16, BLK), F32),
            pltpu.VMEM((ROUNDS, 2 * GROUP, 16, BLK), F32),
            pltpu.VMEM((ROUNDS, far + 1, 16, BLK), F32),
            pltpu.VMEM((4, 8, BLK), F32),
            pltpu.VMEM((ROUNDS, 2, 2 * STEPS, BLK), F32),
            pltpu.SMEM((ROUNDS, n_pairs * SLOTS), jnp.int32),
            dma(()),
            pltpu.SemaphoreType.REGULAR,
            dma((SLOTS,)),
            dma((SLOTS,)),
            dma((ROUNDS, 2)),
            dma((ROUNDS, 2)),
            dma((ROUNDS, near)),
            dma((ROUNDS, near)),
            dma((ROUNDS, far)),
            dma((ROUNDS, far)),
            dma((ROUNDS,)),
            dma((ROUNDS,)),
        ],
        compiler_params=pltpu.CompilerParams(
            collective_id=0, has_side_effects=True, vmem_limit_bytes=60 * 1024 * 1024
        ),
    )(plan, matrix)


def solution(mesh):
    return jax.shard_map(
        functools.partial(on_device, mesh.shape["rows"], mesh.shape["pairs"]),
        mesh=mesh,
        in_specs=(P("rows", "pairs"), P()),
        out_specs=P("rows", "pairs"),
        check_vma=False,
    )
```

```python
import functools

import jax
import jax.numpy as jnp
from jax import lax
from jax.experimental import pallas as pl
from jax.experimental.pallas import tpu as pltpu
from jax.sharding import PartitionSpec as P

MESH = pl.DeviceIdType.MESH
BLK = 128
ROUNDS = 2
STEPS = 4
SLOTS = 4
GROUP = 4
LANES = 128
F32 = jnp.float32
HOPS = ((2, 0), (2, 1), (3, 0), (3, 1), (1, 0), (1, 1), (0, 1))


def roll(x, by):
    return pltpu.roll(x, by % x.shape[1], 1)


def lane_of(shape):
    return lax.broadcasted_iota(jnp.int32, shape, 1)


def pick(x, index):
    return jnp.take_along_axis(x, index, axis=1)


def extra_lanes(slot):
    first = jnp.where(slot < 3, 0, jnp.where(slot < 5, 1, 2))
    second = jnp.where(slot < 3, 2 * slot + 1, jnp.where(slot == 3, 2, jnp.where(slot == 4, 4, 3)))
    return first, jnp.minimum(second, 7)


def band_terms(left, right, reverse):
    lane = lane_of(left.shape)
    top, bottom = left, pick(right, reverse)
    back = pick(left, reverse)
    tops = [top] + [roll(jnp.where(lane < d, right, top), -d) for d in (2, 4, 6)]
    bottoms = [bottom] + [roll(jnp.where(lane < d, back, bottom), -d) for d in (2, 4, 6)]
    first, second = extra_lanes(lane % 8)
    one = jnp.where(lane < 16, pick(top, first), pick(bottom, first))
    two = jnp.where(lane % 16 < 8, pick(top, second), pick(bottom, second))
    terms = [top * t for t in tops] + [top * b for b in bottoms]
    terms += [one * two] + [bottom * t for t in tops[1:]] + [bottom * b for b in bottoms]
    return top, bottom, terms


def fold(x):
    total = x[0:8]
    for first in range(8, x.shape[0], 8):
        total = total + x[first : first + 8]
    return total


def tangent_of(upper_a, lower_b, coupling):
    differ = lower_b - upper_a
    sign_val = jnp.where(differ >= 0.0, 1.0, -1.0)
    denom = jnp.abs(differ) + jnp.sqrt(differ * differ + 4.0 * coupling * coupling)
    positive = denom > 0.0
    safe_den = jnp.where(positive, denom, 1.0)
    return jnp.where(positive, 2.0 * coupling * sign_val / safe_den, 0.0)


def rotate_both(top, bottom, cosine, sine):
    return top * cosine - bottom * sine, top * sine + bottom * cosine


def angles(tt, tb, bt, bb):
    shape = tt.shape
    lane = lane_of(shape)
    row = lax.broadcasted_iota(jnp.int32, shape, 0)
    first, second = extra_lanes(jnp.minimum(lane, 5))
    ahead = lane + 2 * row
    over = ahead > LANES - 1
    is_extra = row == 4
    at_i = jnp.where(is_extra, first, lane)
    at_j = jnp.where(is_extra, second, jnp.where(row > 4, lane, jnp.where(over, 2 * LANES - 1 - ahead, ahead)))
    flip = jnp.where(over & (row < 4), -1.0, 1.0)

    def line(x, r):
        return jnp.broadcast_to(x[r : r + 1], shape)

    def item(x, r, i):
        return jnp.broadcast_to(x[r : r + 1, i : i + 1], shape)

    def up(x):
        return pltpu.roll(x, shape[0] - 1, 0)

    def down(x):
        return pltpu.roll(x, 1, 0)

    cosines, sines = [], []
    for step_no in range(STEPS):
        tangent = tangent_of(line(tt, 0), line(bb, 0), line(tb, 0))
        cosine = 1.0 / jnp.sqrt(1.0 + tangent * tangent)
        sine = cosine * tangent
        cosines.append(cosine[0:1])
        sines.append(sine[0:1])
        if step_no == STEPS - 1:
            break
        cos_i, sin_i = pick(cosine, at_i), pick(sine, at_i)
        cos_j, sin_j = pick(cosine, at_j), pick(sine, at_j) * flip
        tt, tb = rotate_both(tt, tb, cos_j, sin_j)
        bt, bb = rotate_both(bt, bb, cos_j, sin_j)
        tt, bt = rotate_both(tt, bt, cos_i, sin_i)
        tb, bb = rotate_both(tb, bb, cos_i, sin_i)
        new_tt = jnp.where(
            lane >= 2,
            roll(tt, 1),
            jnp.where(
                lane == 1,
                jnp.where(row == 0, roll(bb, 1), roll(bt, 1)),
                jnp.where(row == 0, tt, pick(line(tt, 4), jnp.maximum(row - 1, 0))),
            ),
        )
        new_bb = jnp.where(lane < LANES - 1, roll(bb, -1), pick(tt, LANES - 1 - 2 * row))
        new_tb = jnp.where(
            lane >= 2,
            roll(up(tb), 1),
            jnp.where(lane == 1, roll(up(bb), 1), pick(line(tb, 4), row)),
        )
        new_bt = jnp.where(
            row == 0,
            new_tb,
            jnp.where(
                lane < LANES - 1,
                roll(down(bt), -1),
                pick(down(bt), jnp.minimum(LANES + 1 - 2 * row, LANES - 1)),
            ),
        )
        head = lane == 0
        second_one = lane == 1
        extra_tt = jnp.where(head, item(tb, 0, 0), jnp.where(second_one, item(tt, 1, 0), item(bt, 4, 0)))
        extra_tb = jnp.where(head, item(tb, 1, 0), jnp.where(second_one, item(tb, 2, 0), item(bb, 4, 1)))
        extra_bt = jnp.where(head, item(bb, 4, 0), jnp.where(second_one, item(bt, 4, 3), item(tb, 4, 3)))
        extra_bb = jnp.where(head, item(bb, 4, 3), jnp.where(second_one, item(bb, 4, 4), item(bb, 4, 5)))
        tt = jnp.where(is_extra, extra_tt, new_tt)
        tb = jnp.where(is_extra, extra_tb, new_tb)
        bt = jnp.where(is_extra, extra_bt, new_bt)
        bb = jnp.where(is_extra, extra_bb, new_bb)
    return cosines, sines


def apply_steps(top, bottom, cosines, sines):
    lane = lane_of(top.shape)
    for step_no in range(STEPS):
        top, bottom = rotate_both(top, bottom, cosines[step_no], sines[step_no])
        if step_no < STEPS - 1:
            new_top = jnp.where(lane == 0, top, roll(jnp.where(lane == 0, bottom, top), 1))
            bottom = jnp.where(lane == LANES - 1, top, roll(bottom, -1))
            top = new_top
    last = STEPS - 1
    turn = 2 * LANES - 1 - last
    keep = LANES - last
    left = jnp.where(
        lane == 0,
        top,
        jnp.where(lane < keep, roll(top, -last), pick(bottom, jnp.minimum(turn - lane, LANES - 1))),
    )
    right = jnp.where(
        lane < keep, pick(bottom, jnp.maximum(turn - LANES - lane, 0)), roll(top, LANES - 1 - last)
    )
    return left, right


def kernel(
    n_rows, n_pairs, plan_in, x_ref, o_ref,
    first, second, third, came, sent, cross, crossed, sides, bands, parts, sums, both, entries, turns, far_turns, last_turns,
    plan_ref, plan_sem, ready_sem, in_sem, block_out, block_in, cross_out, cross_in, part_out, part_in,
    sum_out, sum_in, both_out, both_in, turn_out, turn_in,
):
    rows_at = lax.axis_index("rows")
    index = lax.axis_index("pairs")
    z, core = rows_at // 2, rows_at % 2
    n_chips = n_rows // 2
    group, member = z // GROUP, z % GROUP
    local_rows = x_ref.shape[0]

    def device(chip, which_core):
        return (chip * 2 + which_core, index)

    def in_group(step):
        return group * GROUP + (member + step) % GROUP

    ahead = (rows_at, (index + 1) % n_pairs)
    behind = (rows_at, (index + n_pairs - 1) % n_pairs)
    across = jnp.where(member < 2, z + n_chips // 2 + 2, z + n_chips // 2 - 2) % n_chips
    far = (
        across,
        (z + GROUP) % n_chips,
        (z + n_chips - GROUP) % n_chips,
    )
    near = [device(in_group(step), (core + turn) % 2) for step, turn in HOPS]
    line = [device((z + step + n_chips) % n_chips, core) for step in (1, -1, 2, -2)]
    other = device(z, 1 - core)
    peers = line[:2] + [ahead, behind, other]
    barrier = pltpu.get_barrier_semaphore()
    for peer in peers:
        pl.semaphore_signal(barrier, inc=1, device_id=peer, device_id_type=MESH)
    loads = [pltpu.make_async_copy(plan_in, plan_ref, plan_sem)] + [
        pltpu.make_async_copy(
            x_ref.at[:, pl.ds(s * BLK, BLK)], first.at[s], in_sem.at[s]
        )
        for s in range(SLOTS)
    ]
    for load in loads:
        load.start()
    for load in loads:
        load.wait()

    def remote(src, dst, send_sem, recv_sem, to):
        return pltpu.make_async_remote_copy(
            src_ref=src, dst_ref=dst, send_sem=send_sem, recv_sem=recv_sem,
            device_id=to, device_id_type=MESH,
        )

    shape = (8, LANES)
    reverse = LANES - 1 - lane_of((local_rows, LANES))
    started = []
    pl.semaphore_wait(barrier, len(peers))

    def here(level, to):
        for peer in to:
            pl.semaphore_signal(ready_sem.at[level], inc=1, device_id=peer, device_id_type=MESH)

    def known(level):
        pl.semaphore_wait(ready_sem.at[level], 2)

    here(0, line[:2])

    def slots_taken(rnd, at):
        taken = jnp.int32(0)
        for s in range(SLOTS):
            took = plan_ref[rnd, at * SLOTS + s] - index * SLOTS
            taken = jnp.where((took >= 0) & (took < SLOTS), took, taken)
        return taken

    def band_sums(rnd, held, came):
        for pair in range(2):
            blocks = []
            for side in range(2):
                took = plan_ref[rnd, index * SLOTS + 2 * pair + side] - index * SLOTS
                own = held[jnp.clip(took, 0, SLOTS - 1)]
                blocks.append(jnp.where(took < 0, came[0], jnp.where(took >= SLOTS, came[1], own)))
            top, bottom, terms = band_terms(*blocks, reverse)
            sides[pair, 0] = top
            sides[pair, 1] = bottom
            for k in range(16):
                bands[rnd, pair, k : k + 1] = jnp.sum(fold(terms[k]), axis=0, keepdims=True)

    def group_sums(rnd):
        for k, (step, turn) in enumerate(HOPS):
            there = (core + turn) % 2
            copy = remote(
                bands.at[rnd, there], parts.at[rnd, member * 2 + core],
                part_out.at[rnd, k], part_in.at[rnd, k], device(in_group(step), there),
            )
            copy.start()
            started.append(copy)
        parts[rnd, member * 2 + core] = bands[rnd, core]

    def group_total(rnd):
        for k, (step, turn) in enumerate(HOPS):
            source = (in_group(GROUP - step) % GROUP) * 2 + (core + turn) % 2
            remote(
                bands.at[rnd, core], parts.at[rnd, source],
                part_out.at[rnd, k], part_in.at[rnd, k], device(in_group(GROUP - step), (core + turn) % 2),
            ).wait_recv()
        total = parts[rnd, 0]
        for k in range(1, 2 * GROUP):
            total = total + parts[rnd, k]
        return total

    def full_total(ref):
        total = ref[0]
        for k in range(1, n_chips // GROUP):
            total = total + ref[k]
        return total

    def angles_of(total, work):
        work[...] = jnp.zeros(work.shape, F32)
        for k in range(4):
            work[k, 0:4] = total[4 * k : 4 * k + 4]
        work[2, 0:1] = total[4:5]
        for k in range(4):
            work[k, 4:5] = roll(jnp.broadcast_to(total[8:9], shape), -8 * k)[0:1]
        return angles(work[0], work[1], work[2], work[3])

    def spread(x):
        return jnp.broadcast_to(x, (local_rows, LANES))

    def turned(top, bottom, lines):
        wide = [spread(line) for line in lines]
        return apply_steps(top, bottom, wide[:STEPS], wide[STEPS:])

    sent[0] = first[slots_taken(0, ahead[1])]
    sent[1] = first[slots_taken(0, behind[1])]
    moves = [
        remote(sent.at[0], came.at[0], block_out.at[0], block_in.at[0], ahead),
        remote(sent.at[1], came.at[1], block_out.at[1], block_in.at[1], behind),
    ]
    for move in moves:
        move.start()
    known(0)
    here(1, line[2:])
    known(1)
    here(2, line[2:])
    for move in moves:
        move.wait_recv()
    started += moves
    band_sums(0, first, came)
    group_sums(0)

    for way, to in enumerate((ahead, behind)):
        from_second = slots_taken(1, to[1]) >= 2
        for side in range(2):
            cross[way, side] = jnp.where(from_second, sides[1, side], sides[0, side])
        move = remote(cross.at[way], crossed.at[way], cross_out.at[way], cross_in.at[way], to)
        move.start()
        moves.append(move)
    started += moves[2:]

    sums[group] = group_total(0)
    known(2)
    for k, chip in enumerate(far):
        copy = remote(sums.at[group], sums.at[group], sum_out.at[k], sum_in.at[k], device(chip, core))
        copy.start()
        started.append(copy)
    for k, chip in enumerate((far[0], far[2], far[1])):
        remote(
            sums.at[group], sums.at[chip // GROUP], sum_out.at[k], sum_in.at[k], device(chip, core)
        ).wait_recv()
    cosines, sines = angles_of(full_total(sums), entries.at[0])
    for k in range(STEPS):
        turns[core, k : k + 1] = cosines[k]
        turns[core, STEPS + k : STEPS + k + 1] = sines[k]
    for k, (way, there) in enumerate(((0, 0), (0, 1), (1, 0), (1, 1))):
        to = (z * 2 + (core + there) % 2, (ahead, behind)[way][1])
        copy = remote(turns.at[core], far_turns.at[way, core], turn_out.at[k], turn_in.at[k], to)
        copy.start()
        started.append(copy)
    copy = remote(turns.at[core], turns.at[core], turn_out.at[4], turn_in.at[4], other)
    copy.start()
    started.append(copy)
    remote(turns.at[core], turns.at[1 - core], turn_out.at[4], turn_in.at[4], other).wait_recv()
    for pair in range(2):
        lines = [turns[pair, k : k + 1] for k in range(2 * STEPS)]
        left, right = turned(sides[pair, 0], sides[pair, 1], lines)
        second[2 * pair] = left
        second[2 * pair + 1] = right
    for k, (way, there) in enumerate(((0, 0), (0, 1), (1, 0), (1, 1))):
        source = (z * 2 + (core + there) % 2, (behind, ahead)[way][1])
        remote(
            turns.at[core], far_turns.at[way, (core + there) % 2], turn_out.at[k], turn_in.at[k], source
        ).wait_recv()
    for move in moves[2:]:
        move.wait_recv()
    for way in range(2):
        took = jnp.int32(0)
        for s in range(SLOTS):
            at = plan_ref[1, index * SLOTS + s] - index * SLOTS + (SLOTS, -SLOTS)[way]
            took = jnp.where((at >= 0) & (at < SLOTS), at, took)
        lines = [
            jnp.where(took >= 2, far_turns[way, 1, k : k + 1], far_turns[way, 0, k : k + 1])
            for k in range(2 * STEPS)
        ]
        left, right = turned(crossed[way, 0], crossed[way, 1], lines)
        third[way] = jnp.where((took == 1) | (took == 3), right, left)

    band_sums(1, second, third)
    group_sums(1)
    both[group] = group_total(1)
    for k, chip in enumerate(far):
        copy = remote(
            both.at[group], both.at[group], both_out.at[k], both_in.at[k], device(chip, core)
        )
        copy.start()
        started.append(copy)
    for k, chip in enumerate((far[0], far[2], far[1])):
        remote(
            both.at[group], both.at[chip // GROUP], both_out.at[k], both_in.at[k], device(chip, core)
        ).wait_recv()
    cosines, sines = angles_of(full_total(both), entries.at[1])
    for k in range(STEPS):
        last_turns[core, k : k + 1] = cosines[k]
        last_turns[core, STEPS + k : STEPS + k + 1] = sines[k]
    copy = remote(last_turns.at[core], last_turns.at[core], turn_out.at[5], turn_in.at[5], other)
    copy.start()
    started.append(copy)
    remote(last_turns.at[core], last_turns.at[1 - core], turn_out.at[5], turn_in.at[5], other).wait_recv()
    for pair in range(2):
        lines = [last_turns[pair, k : k + 1] for k in range(2 * STEPS)]
        left, right = turned(sides[pair, 0], sides[pair, 1], lines)
        o_ref[:, 2 * pair * BLK : (2 * pair + 1) * BLK] = left
        o_ref[:, (2 * pair + 1) * BLK : (2 * pair + 2) * BLK] = right

    for copy in started:
        copy.wait_send()


def on_device(n_rows, n_pairs, matrix, plan):
    rows, cols = matrix.shape
    dma = pltpu.SemaphoreType.DMA
    near, far = len(HOPS), n_rows // 2 // GROUP - 1
    return pl.pallas_call(
        functools.partial(kernel, n_rows, n_pairs),
        out_shape=pltpu.VMEM((rows, cols), F32),
        in_specs=[
            pl.BlockSpec(memory_space=pl.ANY),
            pl.BlockSpec(memory_space=pl.ANY),
        ],
        out_specs=pl.BlockSpec(memory_space=pltpu.VMEM),
        scratch_shapes=[
            pltpu.VMEM((SLOTS, rows, BLK), F32),
            pltpu.VMEM((SLOTS, rows, BLK), F32),
            pltpu.VMEM((2, rows, BLK), F32),
            pltpu.VMEM((2, rows, BLK), F32),
            pltpu.VMEM((2, rows, BLK), F32),
            pltpu.VMEM((2, 2, rows, BLK), F32),
            pltpu.VMEM((2, 2, rows, BLK), F32),
            pltpu.VMEM((2, 2, rows, BLK), F32),
            pltpu.VMEM((ROUNDS, 2, 16, BLK), F32),
            pltpu.VMEM((ROUNDS, 2 * GROUP, 16, BLK), F32),
            pltpu.VMEM((far + 1, 16, BLK), F32),
            pltpu.VMEM((far + 1, 16, BLK), F32),
            pltpu.VMEM((2, 4, 8, BLK), F32),
            pltpu.VMEM((2, 2 * STEPS, BLK), F32),
            pltpu.VMEM((2, 2, 2 * STEPS, BLK), F32),
            pltpu.VMEM((2, 2 * STEPS, BLK), F32),
            pltpu.SMEM((ROUNDS, n_pairs * SLOTS), jnp.int32),
            dma(()),
            pltpu.SemaphoreType.REGULAR((3,)),
            dma((SLOTS,)),
            dma((2,)),
            dma((2,)),
            dma((2,)),
            dma((2,)),
            dma((ROUNDS, near)),
            dma((ROUNDS, near)),
            dma((far,)),
            dma((far,)),
            dma((far,)),
            dma((far,)),
            dma((6,)),
            dma((6,)),
        ],
        compiler_params=pltpu.CompilerParams(
            collective_id=0, has_side_effects=True, vmem_limit_bytes=60 * 1024 * 1024
        ),
    )(plan, matrix)


def solution(mesh):
    return jax.shard_map(
        functools.partial(on_device, mesh.shape["rows"], mesh.shape["pairs"]),
        mesh=mesh,
        in_specs=(P("rows", "pairs"), P()),
        out_specs=P("rows", "pairs"),
        check_vma=False,
    )
```

```python
import functools

import jax
import jax.numpy as jnp
from jax import lax
from jax.experimental import pallas as pl
from jax.experimental.pallas import tpu as pltpu
from jax.sharding import PartitionSpec as P

MESH = pl.DeviceIdType.MESH
BLK = 128
ROUNDS = 2
STEPS = 4
SLOTS = 4
GROUP = 4
LANES = 128
ENTRIES = 16
F32 = jnp.float32
HOPS = ((3, 0), (3, 1), (2, 0), (2, 1), (1, 0), (1, 1), (0, 1))


def roll(x, by):
    return pltpu.roll(x, by % x.shape[1], 1)


def lane_of(shape):
    return lax.broadcasted_iota(jnp.int32, shape, 1)


def pick(x, index):
    return jnp.take_along_axis(x, index, axis=1)


def extra_lanes(slot):
    first = jnp.where(slot < 3, 0, jnp.where(slot < 5, 1, 2))
    second = jnp.where(slot < 3, 2 * slot + 1, jnp.where(slot == 3, 2, jnp.where(slot == 4, 4, 3)))
    return first, jnp.minimum(second, 7)


def band_terms(left, right, reverse):
    lane = lane_of(left.shape)
    top, bottom = left, pick(right, reverse)
    back = pick(left, reverse)
    tops = [top] + [roll(jnp.where(lane < d, right, top), -d) for d in (2, 4, 6)]
    bottoms = [bottom] + [roll(jnp.where(lane < d, back, bottom), -d) for d in (2, 4, 6)]
    first, second = extra_lanes(lane % 8)
    one = jnp.where(lane < 16, pick(top, first), pick(bottom, first))
    two = jnp.where(lane % 16 < 8, pick(top, second), pick(bottom, second))
    terms = [top * t for t in tops] + [top * b for b in bottoms]
    terms += [one * two] + [bottom * t for t in tops[1:]] + [bottom * b for b in bottoms]
    return top, bottom, terms


def fold(x):
    total = x[0:8]
    for first in range(8, x.shape[0], 8):
        total = total + x[first : first + 8]
    return total


def tangent_of(upper_a, lower_b, coupling):
    differ = lower_b - upper_a
    sign_val = jnp.where(differ >= 0.0, 1.0, -1.0)
    denom = jnp.abs(differ) + jnp.sqrt(differ * differ + 4.0 * coupling * coupling)
    positive = denom > 0.0
    safe_den = jnp.where(positive, denom, 1.0)
    return jnp.where(positive, 2.0 * coupling * sign_val / safe_den, 0.0)


def rotate_both(top, bottom, cosine, sine):
    return top * cosine - bottom * sine, top * sine + bottom * cosine


def angles(tt, tb, bt, bb):
    shape = tt.shape
    lane = lane_of(shape)
    row = lax.broadcasted_iota(jnp.int32, shape, 0)
    first, second = extra_lanes(jnp.minimum(lane, 5))
    ahead = lane + 2 * row
    over = ahead > LANES - 1
    is_extra = row == 4
    at_i = jnp.where(is_extra, first, lane)
    at_j = jnp.where(is_extra, second, jnp.where(row > 4, lane, jnp.where(over, 2 * LANES - 1 - ahead, ahead)))
    flip = jnp.where(over & (row < 4), -1.0, 1.0)

    def line(x, r):
        return jnp.broadcast_to(x[r : r + 1], shape)

    def item(x, r, i):
        return jnp.broadcast_to(x[r : r + 1, i : i + 1], shape)

    def up(x):
        return pltpu.roll(x, shape[0] - 1, 0)

    def down(x):
        return pltpu.roll(x, 1, 0)

    cosines, sines = [], []
    for step_no in range(STEPS):
        tangent = tangent_of(line(tt, 0), line(bb, 0), line(tb, 0))
        cosine = 1.0 / jnp.sqrt(1.0 + tangent * tangent)
        sine = cosine * tangent
        cosines.append(cosine[0:1])
        sines.append(sine[0:1])
        if step_no == STEPS - 1:
            break
        cos_i, sin_i = pick(cosine, at_i), pick(sine, at_i)
        cos_j, sin_j = pick(cosine, at_j), pick(sine, at_j) * flip
        tt, tb = rotate_both(tt, tb, cos_j, sin_j)
        bt, bb = rotate_both(bt, bb, cos_j, sin_j)
        tt, bt = rotate_both(tt, bt, cos_i, sin_i)
        tb, bb = rotate_both(tb, bb, cos_i, sin_i)
        new_tt = jnp.where(
            lane >= 2,
            roll(tt, 1),
            jnp.where(
                lane == 1,
                jnp.where(row == 0, roll(bb, 1), roll(bt, 1)),
                jnp.where(row == 0, tt, pick(line(tt, 4), jnp.maximum(row - 1, 0))),
            ),
        )
        new_bb = jnp.where(lane < LANES - 1, roll(bb, -1), pick(tt, LANES - 1 - 2 * row))
        new_tb = jnp.where(
            lane >= 2,
            roll(up(tb), 1),
            jnp.where(lane == 1, roll(up(bb), 1), pick(line(tb, 4), row)),
        )
        new_bt = jnp.where(
            row == 0,
            new_tb,
            jnp.where(
                lane < LANES - 1,
                roll(down(bt), -1),
                pick(down(bt), jnp.minimum(LANES + 1 - 2 * row, LANES - 1)),
            ),
        )
        head = lane == 0
        second_one = lane == 1
        extra_tt = jnp.where(head, item(tb, 0, 0), jnp.where(second_one, item(tt, 1, 0), item(bt, 4, 0)))
        extra_tb = jnp.where(head, item(tb, 1, 0), jnp.where(second_one, item(tb, 2, 0), item(bb, 4, 1)))
        extra_bt = jnp.where(head, item(bb, 4, 0), jnp.where(second_one, item(bt, 4, 3), item(tb, 4, 3)))
        extra_bb = jnp.where(head, item(bb, 4, 3), jnp.where(second_one, item(bb, 4, 4), item(bb, 4, 5)))
        tt = jnp.where(is_extra, extra_tt, new_tt)
        tb = jnp.where(is_extra, extra_tb, new_tb)
        bt = jnp.where(is_extra, extra_bt, new_bt)
        bb = jnp.where(is_extra, extra_bb, new_bb)
    return cosines, sines


def apply_steps(top, bottom, cosines, sines):
    lane = lane_of(top.shape)
    for step_no in range(STEPS):
        top, bottom = rotate_both(top, bottom, cosines[step_no], sines[step_no])
        if step_no < STEPS - 1:
            new_top = jnp.where(lane == 0, top, roll(jnp.where(lane == 0, bottom, top), 1))
            bottom = jnp.where(lane == LANES - 1, top, roll(bottom, -1))
            top = new_top
    last = STEPS - 1
    turn = 2 * LANES - 1 - last
    keep = LANES - last
    left = jnp.where(
        lane == 0,
        top,
        jnp.where(lane < keep, roll(top, -last), pick(bottom, jnp.minimum(turn - lane, LANES - 1))),
    )
    right = jnp.where(
        lane < keep, pick(bottom, jnp.maximum(turn - LANES - lane, 0)), roll(top, LANES - 1 - last)
    )
    return left, right


def kernel(
    n_rows, n_pairs, plan_in, x_ref, o_ref,
    first, second, third, came, sent, cross, crossed, sides, bands, parts, sums, entries, turns, far_turns, last_turns,
    plan_ref, plan_sem, ready_sem, in_sem, block_out, block_in, cross_out, cross_in, part_out, part_in,
    sum_out, sum_in, turn_out, turn_in,
):
    rows_at = lax.axis_index("rows")
    index = lax.axis_index("pairs")
    z, core = rows_at // 2, rows_at % 2
    n_chips = n_rows // 2
    group, member = z // GROUP, z % GROUP
    local_rows = x_ref.shape[0]

    def device(chip, which_core):
        return (chip * 2 + which_core, index)

    partner = [
        group * GROUP + at
        for at in (member, member + 1 - 2 * (member % 2), (member + 2) % GROUP, GROUP - 1 - member)
    ]
    near = [(which * 2 + turn, (core + turn) % 2, device(partner[which], (core + turn) % 2)) for which, turn in HOPS]
    near_slot = [
        ((member // 2 + at // 2) % 2 * 2 + (member + at) % 2) * 2 + (core + which_core) % 2
        for at in range(GROUP)
        for which_core in range(2)
    ]
    ahead = (rows_at, (index + 1) % n_pairs)
    behind = (rows_at, (index + n_pairs - 1) % n_pairs)
    across = jnp.where(member < 2, z + n_chips // 2 + 2, z + n_chips // 2 - 2) % n_chips
    n_groups = n_chips // GROUP
    far = [(2, device(across, core)), (3, device((z + GROUP) % n_chips, core)), (1, device((z + n_chips - GROUP) % n_chips, core))]
    far_slot = [(at + n_groups - group) % n_groups for at in range(n_groups)]
    both_cores = [
        (way, (rows_at if turn == 0 else z * 2 + 1 - core, to[1]))
        for way, to in enumerate((ahead, behind))
        for turn in (0, 1)
    ]
    line = [device((z + step + n_chips) % n_chips, core) for step in (1, -1, 2, -2)]
    other = device(z, 1 - core)
    peers = line[:2] + [ahead, behind, other]
    barrier = pltpu.get_barrier_semaphore()
    for peer in peers:
        pl.semaphore_signal(barrier, inc=1, device_id=peer, device_id_type=MESH)
    loads = [pltpu.make_async_copy(plan_in, plan_ref, plan_sem)] + [
        pltpu.make_async_copy(
            x_ref.at[:, pl.ds(s * BLK, BLK)], first.at[s], in_sem.at[s]
        )
        for s in range(SLOTS)
    ]
    for load in loads:
        load.start()
    for load in loads:
        load.wait()

    def remote(src, dst, send_sem, recv_sem, to):
        return pltpu.make_async_remote_copy(
            src_ref=src, dst_ref=dst, send_sem=send_sem, recv_sem=recv_sem,
            device_id=to, device_id_type=MESH,
        )

    shape = (8, LANES)
    reverse = LANES - 1 - lane_of((local_rows, LANES))
    pl.semaphore_wait(barrier, len(peers))

    def here(level, to):
        for peer in to:
            pl.semaphore_signal(ready_sem.at[level], inc=1, device_id=peer, device_id_type=MESH)

    def known(level):
        pl.semaphore_wait(ready_sem.at[level], 2)

    here(0, line[:2])

    def slots_taken(rnd, at):
        taken = jnp.int32(0)
        for s in range(SLOTS):
            took = plan_ref[rnd, at * SLOTS + s] - index * SLOTS
            taken = jnp.where((took >= 0) & (took < SLOTS), took, taken)
        return taken

    def band_sums(rnd, held, came):
        for pair in range(2):
            blocks = []
            for side in range(2):
                took = plan_ref[rnd, index * SLOTS + 2 * pair + side] - index * SLOTS
                own = held[jnp.clip(took, 0, SLOTS - 1)]
                blocks.append(jnp.where(took < 0, came[0], jnp.where(took >= SLOTS, came[1], own)))
            top, bottom, terms = band_terms(*blocks, reverse)
            sides[pair, 0] = top
            sides[pair, 1] = bottom
            for k in range(16):
                bands[rnd, pair, k : k + 1] = jnp.sum(fold(terms[k]), axis=0, keepdims=True)

    def wait_all(refs, send_sem, recv_sem):
        return remote(refs, refs, send_sem, recv_sem, other)

    def send_near(rnd):
        for slot, there, to in near:
            remote(
                bands.at[rnd, there], parts.at[rnd, slot], part_out.at[rnd], part_in.at[rnd], to
            ).start()
        parts[rnd, 0] = bands[rnd, core]
        return wait_all(parts.at[rnd, pl.ds(1, len(near))], part_out.at[rnd], part_in.at[rnd])

    def sum_rows(rnd, near_copies):
        near_copies.wait_recv()
        sums[rnd, 0] = in_order(parts.at[rnd], near_slot)
        if rnd == 0:
            known(2)
        for slot, to in far:
            remote(sums.at[rnd, 0], sums.at[rnd, slot], sum_out.at[rnd], sum_in.at[rnd], to).start()
        copies = wait_all(sums.at[rnd, pl.ds(1, len(far))], sum_out.at[rnd], sum_in.at[rnd])
        near_copies.wait_send()
        copies.wait_recv()
        total = in_order(sums.at[rnd], far_slot)
        return total, copies

    def in_order(ref, slots):
        total = ref[slots[0]]
        for slot in slots[1:]:
            total = total + ref[slot]
        return total

    def angles_of(total, work):
        work[...] = jnp.zeros(work.shape, F32)
        for k in range(4):
            work[k, 0:4] = total[4 * k : 4 * k + 4]
        work[2, 0:1] = total[4:5]
        for k in range(4):
            work[k, 4:5] = roll(jnp.broadcast_to(total[8:9], shape), -8 * k)[0:1]
        return angles(work[0], work[1], work[2], work[3])

    def spread(x):
        return jnp.broadcast_to(x, (local_rows, LANES))

    def turned(top, bottom, lines):
        wide = [spread(line) for line in lines]
        return apply_steps(top, bottom, wide[:STEPS], wide[STEPS:])

    for way, to in enumerate((ahead, behind)):
        sent[way] = first[slots_taken(0, to[1])]
        remote(sent.at[way], came.at[way], block_out, block_in, to).start()
    blocks = wait_all(came, block_out, block_in)
    known(0)
    here(1, line[2:])
    known(1)
    here(2, line[2:])
    blocks.wait_recv()
    band_sums(0, first, came)
    near_copies = send_near(0)

    for way, to in enumerate((ahead, behind)):
        from_second = slots_taken(1, to[1]) >= 2
        for side in range(2):
            cross[way, side] = jnp.where(from_second, sides[1, side], sides[0, side])
        remote(cross.at[way], crossed.at[way], cross_out, cross_in, to).start()
    columns = wait_all(crossed, cross_out, cross_in)
    blocks.wait_send()

    total, far_copies = sum_rows(0, near_copies)
    cosines, sines = angles_of(total, entries.at[0])
    for k in range(STEPS):
        turns[core, k : k + 1] = cosines[k]
        turns[core, STEPS + k : STEPS + k + 1] = sines[k]
    for way, to in both_cores:
        remote(turns.at[core], far_turns.at[way, core], turn_out.at[0], turn_in.at[0], to).start()
    far_angles = wait_all(far_turns, turn_out.at[0], turn_in.at[0])
    remote(turns.at[core], turns.at[core], turn_out.at[1], turn_in.at[1], other).start()
    angles_here = wait_all(turns.at[1 - core], turn_out.at[1], turn_in.at[1])
    far_copies.wait_send()
    columns.wait_send()
    angles_here.wait_recv()
    for pair in range(2):
        lines = [turns[pair, k : k + 1] for k in range(2 * STEPS)]
        left, right = turned(sides[pair, 0], sides[pair, 1], lines)
        second[2 * pair] = left
        second[2 * pair + 1] = right
    columns.wait_recv()
    far_angles.wait_recv()
    for way in range(2):
        took = jnp.int32(0)
        for s in range(SLOTS):
            at = plan_ref[1, index * SLOTS + s] - index * SLOTS + (SLOTS, -SLOTS)[way]
            took = jnp.where((at >= 0) & (at < SLOTS), at, took)
        lines = [
            jnp.where(took >= 2, far_turns[way, 1, k : k + 1], far_turns[way, 0, k : k + 1])
            for k in range(2 * STEPS)
        ]
        left, right = turned(crossed[way, 0], crossed[way, 1], lines)
        third[way] = jnp.where((took == 1) | (took == 3), right, left)

    band_sums(1, second, third)
    near_copies = send_near(1)
    far_angles.wait_send()
    angles_here.wait_send()
    total, far_copies = sum_rows(1, near_copies)
    cosines, sines = angles_of(total, entries.at[1])
    for k in range(STEPS):
        last_turns[core, k : k + 1] = cosines[k]
        last_turns[core, STEPS + k : STEPS + k + 1] = sines[k]
    remote(last_turns.at[core], last_turns.at[core], turn_out.at[2], turn_in.at[2], other).start()
    angles_here = wait_all(last_turns.at[1 - core], turn_out.at[2], turn_in.at[2])
    far_copies.wait_send()
    angles_here.wait_recv()
    for pair in range(2):
        lines = [last_turns[pair, k : k + 1] for k in range(2 * STEPS)]
        left, right = turned(sides[pair, 0], sides[pair, 1], lines)
        o_ref[:, 2 * pair * BLK : (2 * pair + 1) * BLK] = left
        o_ref[:, (2 * pair + 1) * BLK : (2 * pair + 2) * BLK] = right

    angles_here.wait_send()


def on_device(n_rows, n_pairs, matrix, plan):
    rows, cols = matrix.shape
    dma = pltpu.SemaphoreType.DMA
    return pl.pallas_call(
        functools.partial(kernel, n_rows, n_pairs),
        out_shape=pltpu.VMEM((rows, cols), F32),
        in_specs=[
            pl.BlockSpec(memory_space=pl.ANY),
            pl.BlockSpec(memory_space=pl.ANY),
        ],
        out_specs=pl.BlockSpec(memory_space=pltpu.VMEM),
        scratch_shapes=[
            pltpu.VMEM((SLOTS, rows, BLK), F32),
            pltpu.VMEM((SLOTS, rows, BLK), F32),
            pltpu.VMEM((2, rows, BLK), F32),
            pltpu.VMEM((2, rows, BLK), F32),
            pltpu.VMEM((2, rows, BLK), F32),
            pltpu.VMEM((2, 2, rows, BLK), F32),
            pltpu.VMEM((2, 2, rows, BLK), F32),
            pltpu.VMEM((2, 2, rows, BLK), F32),
            pltpu.VMEM((ROUNDS, 2, ENTRIES, BLK), F32),
            pltpu.VMEM((ROUNDS, 2 * GROUP, ENTRIES, BLK), F32),
            pltpu.VMEM((ROUNDS, n_rows // 2 // GROUP, ENTRIES, BLK), F32),
            pltpu.VMEM((2, 4, 8, BLK), F32),
            pltpu.VMEM((2, 2 * STEPS, BLK), F32),
            pltpu.VMEM((2, 2, 2 * STEPS, BLK), F32),
            pltpu.VMEM((2, 2 * STEPS, BLK), F32),
            pltpu.SMEM((ROUNDS, n_pairs * SLOTS), jnp.int32),
            dma(()),
            pltpu.SemaphoreType.REGULAR((3,)),
            dma((SLOTS,)),
            dma(()),
            dma(()),
            dma(()),
            dma(()),
            dma((ROUNDS,)),
            dma((ROUNDS,)),
            dma((ROUNDS,)),
            dma((ROUNDS,)),
            dma((3,)),
            dma((3,)),
        ],
        compiler_params=pltpu.CompilerParams(
            collective_id=0, has_side_effects=True, vmem_limit_bytes=60 * 1024 * 1024
        ),
    )(plan, matrix)


def solution(mesh):
    return jax.shard_map(
        functools.partial(on_device, mesh.shape["rows"], mesh.shape["pairs"]),
        mesh=mesh,
        in_specs=(P("rows", "pairs"), P()),
        out_specs=P("rows", "pairs"),
        check_vma=False,
    )
```

```python
import functools

import jax
import jax.numpy as jnp
from jax import lax
from jax.experimental import pallas as pl
from jax.experimental.pallas import tpu as pltpu
from jax.sharding import PartitionSpec as P

MESH = pl.DeviceIdType.MESH
BLK = 128
ROUNDS = 2
STEPS = 4
SLOTS = 4
GROUP = 4
LANES = 128
ENTRIES = 16
F32 = jnp.float32
HOPS = ((3, 0), (3, 1), (2, 0), (2, 1), (1, 0), (1, 1), (0, 1))


def roll(x, by):
    return pltpu.roll(x, by % x.shape[1], 1)


def lane_of(shape):
    return lax.broadcasted_iota(jnp.int32, shape, 1)


def pick(x, index):
    return jnp.take_along_axis(x, index, axis=1)


def extra_lanes(slot):
    first = jnp.where(slot < 3, 0, jnp.where(slot < 5, 1, 2))
    second = jnp.where(slot < 3, 2 * slot + 1, jnp.where(slot == 3, 2, jnp.where(slot == 4, 4, 3)))
    return first, jnp.minimum(second, 7)


def band_terms(left, right, reverse):
    lane = lane_of(left.shape)
    top, bottom = left, pick(right, reverse)
    back = pick(left, reverse)
    tops = [top] + [roll(jnp.where(lane < d, right, top), -d) for d in (2, 4, 6)]
    bottoms = [bottom] + [roll(jnp.where(lane < d, back, bottom), -d) for d in (2, 4, 6)]
    first, second = extra_lanes(lane % 8)
    one = jnp.where(lane < 16, pick(top, first), pick(bottom, first))
    two = jnp.where(lane % 16 < 8, pick(top, second), pick(bottom, second))
    terms = [top * t for t in tops] + [top * b for b in bottoms]
    terms += [one * two] + [bottom * t for t in tops[1:]] + [bottom * b for b in bottoms]
    return top, bottom, terms


def fold(x):
    total = x[0:8]
    for first in range(8, x.shape[0], 8):
        total = total + x[first : first + 8]
    return total


def tangent_of(upper_a, lower_b, coupling):
    differ = lower_b - upper_a
    sign_val = jnp.where(differ >= 0.0, 1.0, -1.0)
    denom = jnp.abs(differ) + jnp.sqrt(differ * differ + 4.0 * coupling * coupling)
    positive = denom > 0.0
    safe_den = jnp.where(positive, denom, 1.0)
    return jnp.where(positive, 2.0 * coupling * sign_val / safe_den, 0.0)


def rotate_both(top, bottom, cosine, sine):
    return top * cosine - bottom * sine, top * sine + bottom * cosine


def angles(tt, tb, bt, bb):
    shape = tt.shape
    lane = lane_of(shape)
    row = lax.broadcasted_iota(jnp.int32, shape, 0)
    first, second = extra_lanes(jnp.minimum(lane, 5))
    ahead = lane + 2 * row
    over = ahead > LANES - 1
    is_extra = row == 4
    at_i = jnp.where(is_extra, first, lane)
    at_j = jnp.where(is_extra, second, jnp.where(row > 4, lane, jnp.where(over, 2 * LANES - 1 - ahead, ahead)))
    flip = jnp.where(over & (row < 4), -1.0, 1.0)

    def line(x, r):
        return jnp.broadcast_to(x[r : r + 1], shape)

    def item(x, r, i):
        return jnp.broadcast_to(x[r : r + 1, i : i + 1], shape)

    def up(x):
        return pltpu.roll(x, shape[0] - 1, 0)

    def down(x):
        return pltpu.roll(x, 1, 0)

    cosines, sines = [], []
    for step_no in range(STEPS):
        tangent = tangent_of(line(tt, 0), line(bb, 0), line(tb, 0))
        cosine = 1.0 / jnp.sqrt(1.0 + tangent * tangent)
        sine = cosine * tangent
        cosines.append(cosine[0:1])
        sines.append(sine[0:1])
        if step_no == STEPS - 1:
            break
        cos_i, sin_i = pick(cosine, at_i), pick(sine, at_i)
        cos_j, sin_j = pick(cosine, at_j), pick(sine, at_j) * flip
        tt, tb = rotate_both(tt, tb, cos_j, sin_j)
        bt, bb = rotate_both(bt, bb, cos_j, sin_j)
        tt, bt = rotate_both(tt, bt, cos_i, sin_i)
        tb, bb = rotate_both(tb, bb, cos_i, sin_i)
        new_tt = jnp.where(
            lane >= 2,
            roll(tt, 1),
            jnp.where(
                lane == 1,
                jnp.where(row == 0, roll(bb, 1), roll(bt, 1)),
                jnp.where(row == 0, tt, pick(line(tt, 4), jnp.maximum(row - 1, 0))),
            ),
        )
        new_bb = jnp.where(lane < LANES - 1, roll(bb, -1), pick(tt, LANES - 1 - 2 * row))
        new_tb = jnp.where(
            lane >= 2,
            roll(up(tb), 1),
            jnp.where(lane == 1, roll(up(bb), 1), pick(line(tb, 4), row)),
        )
        new_bt = jnp.where(
            row == 0,
            new_tb,
            jnp.where(
                lane < LANES - 1,
                roll(down(bt), -1),
                pick(down(bt), jnp.minimum(LANES + 1 - 2 * row, LANES - 1)),
            ),
        )
        head = lane == 0
        second_one = lane == 1
        extra_tt = jnp.where(head, item(tb, 0, 0), jnp.where(second_one, item(tt, 1, 0), item(bt, 4, 0)))
        extra_tb = jnp.where(head, item(tb, 1, 0), jnp.where(second_one, item(tb, 2, 0), item(bb, 4, 1)))
        extra_bt = jnp.where(head, item(bb, 4, 0), jnp.where(second_one, item(bt, 4, 3), item(tb, 4, 3)))
        extra_bb = jnp.where(head, item(bb, 4, 3), jnp.where(second_one, item(bb, 4, 4), item(bb, 4, 5)))
        tt = jnp.where(is_extra, extra_tt, new_tt)
        tb = jnp.where(is_extra, extra_tb, new_tb)
        bt = jnp.where(is_extra, extra_bt, new_bt)
        bb = jnp.where(is_extra, extra_bb, new_bb)
    return cosines, sines


def apply_steps(top, bottom, cosines, sines):
    lane = lane_of(top.shape)
    for step_no in range(STEPS):
        top, bottom = rotate_both(top, bottom, cosines[step_no], sines[step_no])
        if step_no < STEPS - 1:
            new_top = jnp.where(lane == 0, top, roll(jnp.where(lane == 0, bottom, top), 1))
            bottom = jnp.where(lane == LANES - 1, top, roll(bottom, -1))
            top = new_top
    last = STEPS - 1
    turn = 2 * LANES - 1 - last
    keep = LANES - last
    left = jnp.where(
        lane == 0,
        top,
        jnp.where(lane < keep, roll(top, -last), pick(bottom, jnp.minimum(turn - lane, LANES - 1))),
    )
    right = jnp.where(
        lane < keep, pick(bottom, jnp.maximum(turn - LANES - lane, 0)), roll(top, LANES - 1 - last)
    )
    return left, right


def kernel(
    n_rows, n_pairs, plan_in, x_ref, o_ref,
    first, second, third, came, sent, cross, crossed, sides, bands, parts, sums, entries, turns, far_turns, last_turns,
    plan_ref, plan_sem, ready_sem, in_sem, block_out, block_in, cross_out, cross_in, part_out, part_in,
    sum_out, sum_in, far_turn_out, far_turn_in, turn_out, turn_in,
):
    rows_at = lax.axis_index("rows")
    index = lax.axis_index("pairs")
    z, core = rows_at // 2, rows_at % 2
    n_chips = n_rows // 2
    group, member = z // GROUP, z % GROUP
    local_rows = x_ref.shape[0]

    def device(chip, which_core):
        return (chip * 2 + which_core, index)

    partner = [
        group * GROUP + at
        for at in (member, member + 1 - 2 * (member % 2), (member + 2) % GROUP, GROUP - 1 - member)
    ]
    near = [(which * 2 + turn, (core + turn) % 2, device(partner[which], (core + turn) % 2)) for which, turn in HOPS]
    near_slot = [
        ((member // 2 + at // 2) % 2 * 2 + (member + at) % 2) * 2 + (core + which_core) % 2
        for at in range(GROUP)
        for which_core in range(2)
    ]
    ahead = (rows_at, (index + 1) % n_pairs)
    behind = (rows_at, (index + n_pairs - 1) % n_pairs)
    across = jnp.where(member < 2, z + n_chips // 2 + 2, z + n_chips // 2 - 2) % n_chips
    n_groups = n_chips // GROUP
    far = [(2, device(across, core)), (3, device((z + GROUP) % n_chips, core)), (1, device((z + n_chips - GROUP) % n_chips, core))]
    far_slot = [(at + n_groups - group) % n_groups for at in range(n_groups)]
    has = (index < n_pairs - 1, index > 0)
    sides_here = has[::-1]
    line = [device((z + step + n_chips) % n_chips, core) for step in (1, -1, 2, -2)]
    other = device(z, 1 - core)
    peers = line[:2] + [other]
    barrier = pltpu.get_barrier_semaphore()
    for peer in peers:
        pl.semaphore_signal(barrier, inc=1, device_id=peer, device_id_type=MESH)
    for there, peer in zip(has, (ahead, behind)):

        @pl.when(there)
        def greet(peer=peer):
            pl.semaphore_signal(barrier, inc=1, device_id=peer, device_id_type=MESH)

    loads = [pltpu.make_async_copy(plan_in, plan_ref, plan_sem)] + [
        pltpu.make_async_copy(
            x_ref.at[:, pl.ds(s * BLK, BLK)], first.at[s], in_sem.at[s]
        )
        for s in range(SLOTS)
    ]
    for load in loads:
        load.start()
    for load in loads:
        load.wait()

    def remote(src, dst, send_sem, recv_sem, to):
        return pltpu.make_async_remote_copy(
            src_ref=src, dst_ref=dst, send_sem=send_sem, recv_sem=recv_sem,
            device_id=to, device_id_type=MESH,
        )

    shape = (8, LANES)
    reverse = LANES - 1 - lane_of((local_rows, LANES))
    pl.semaphore_wait(barrier, len(peers) + 2 - (index == 0) - (index == n_pairs - 1))

    def here(level, to):
        for peer in to:
            pl.semaphore_signal(ready_sem.at[level], inc=1, device_id=peer, device_id_type=MESH)

    def known(level):
        pl.semaphore_wait(ready_sem.at[level], 2)

    here(0, line[:2])

    def slots_taken(rnd, at):
        taken = jnp.int32(0)
        for s in range(SLOTS):
            took = plan_ref[rnd, at * SLOTS + s] - index * SLOTS
            taken = jnp.where((took >= 0) & (took < SLOTS), took, taken)
        return taken

    def band_sums(rnd, held, came):
        for pair in range(2):
            blocks = []
            for side in range(2):
                took = plan_ref[rnd, index * SLOTS + 2 * pair + side] - index * SLOTS
                own = held[jnp.clip(took, 0, SLOTS - 1)]
                blocks.append(jnp.where(took < 0, came[0], jnp.where(took >= SLOTS, came[1], own)))
            top, bottom, terms = band_terms(*blocks, reverse)
            sides[pair, 0] = top
            sides[pair, 1] = bottom
            for k in range(16):
                bands[rnd, pair, k : k + 1] = jnp.sum(fold(terms[k]), axis=0, keepdims=True)

    def wait_all(refs, send_sem, recv_sem):
        return remote(refs, refs, send_sem, recv_sem, other)

    def send_near(rnd):
        for slot, there, to in near:
            remote(
                bands.at[rnd, there], parts.at[rnd, slot], part_out.at[rnd], part_in.at[rnd], to
            ).start()
        parts[rnd, 0] = bands[rnd, core]
        return wait_all(parts.at[rnd, pl.ds(1, len(near))], part_out.at[rnd], part_in.at[rnd])

    def sum_rows(rnd, near_copies):
        near_copies.wait_recv()
        sums[rnd, 0] = in_order(parts.at[rnd], near_slot)
        if rnd == 0:
            known(2)
        for slot, to in far:
            remote(sums.at[rnd, 0], sums.at[rnd, slot], sum_out.at[rnd], sum_in.at[rnd], to).start()
        copies = wait_all(sums.at[rnd, pl.ds(1, len(far))], sum_out.at[rnd], sum_in.at[rnd])
        near_copies.wait_send()
        copies.wait_recv()
        total = in_order(sums.at[rnd], far_slot)
        return total, copies

    def in_order(ref, slots):
        total = ref[slots[0]]
        for slot in slots[1:]:
            total = total + ref[slot]
        return total

    def angles_of(total, work):
        work[...] = jnp.zeros(work.shape, F32)
        for k in range(4):
            work[k, 0:4] = total[4 * k : 4 * k + 4]
        work[2, 0:1] = total[4:5]
        for k in range(4):
            work[k, 4:5] = roll(jnp.broadcast_to(total[8:9], shape), -8 * k)[0:1]
        return angles(work[0], work[1], work[2], work[3])

    def spread(x):
        return jnp.broadcast_to(x, (local_rows, LANES))

    def turned(top, bottom, lines):
        wide = [spread(line) for line in lines]
        return apply_steps(top, bottom, wide[:STEPS], wide[STEPS:])

    def exchange(pairs_of_refs, send_sem, recv_sem):
        for way, to in enumerate((ahead, behind)):

            @pl.when(has[way])
            def start(way=way, to=to):
                for src, dst, which_core in pairs_of_refs(way):
                    device_to = (z * 2 + which_core, to[1])
                    remote(src, dst, send_sem.at[way], recv_sem.at[way], device_to).start()

        def wait(ref, received):
            for way in range(2):

                @pl.when(sides_here[way] if received else has[way])
                def one(way=way):
                    copy = wait_all(ref.at[way], send_sem.at[way], recv_sem.at[way])
                    if received:
                        copy.wait_recv()
                    else:
                        copy.wait_send()

        return wait

    for way, to in enumerate((ahead, behind)):
        sent[way] = first[slots_taken(0, to[1])]
    blocks = exchange(lambda way: [(sent.at[way], came.at[way], core)], block_out, block_in)
    known(0)
    here(1, line[2:])
    known(1)
    here(2, line[2:])
    blocks(came, True)
    band_sums(0, first, came)
    near_copies = send_near(0)

    for way, to in enumerate((ahead, behind)):
        from_second = slots_taken(1, to[1]) >= 2
        for side in range(2):
            cross[way, side] = jnp.where(from_second, sides[1, side], sides[0, side])
    columns = exchange(lambda way: [(cross.at[way], crossed.at[way], core)], cross_out, cross_in)
    blocks(came, False)

    total, far_copies = sum_rows(0, near_copies)
    cosines, sines = angles_of(total, entries.at[0])
    for k in range(STEPS):
        turns[core, k : k + 1] = cosines[k]
        turns[core, STEPS + k : STEPS + k + 1] = sines[k]
    far_angles = exchange(
        lambda way: [(turns.at[core], far_turns.at[way, core], which) for which in (core, 1 - core)],
        far_turn_out, far_turn_in,
    )
    remote(turns.at[core], turns.at[core], turn_out.at[1], turn_in.at[1], other).start()
    angles_here = wait_all(turns.at[1 - core], turn_out.at[1], turn_in.at[1])
    far_copies.wait_send()
    columns(crossed, False)
    angles_here.wait_recv()
    for pair in range(2):
        lines = [turns[pair, k : k + 1] for k in range(2 * STEPS)]
        left, right = turned(sides[pair, 0], sides[pair, 1], lines)
        second[2 * pair] = left
        second[2 * pair + 1] = right
    columns(crossed, True)
    far_angles(far_turns, True)
    for way in range(2):
        took = jnp.int32(0)
        for s in range(SLOTS):
            at = plan_ref[1, index * SLOTS + s] - index * SLOTS + (SLOTS, -SLOTS)[way]
            took = jnp.where((at >= 0) & (at < SLOTS), at, took)
        lines = [
            jnp.where(took >= 2, far_turns[way, 1, k : k + 1], far_turns[way, 0, k : k + 1])
            for k in range(2 * STEPS)
        ]
        left, right = turned(crossed[way, 0], crossed[way, 1], lines)
        third[way] = jnp.where((took == 1) | (took == 3), right, left)

    band_sums(1, second, third)
    near_copies = send_near(1)
    far_angles(far_turns, False)
    angles_here.wait_send()
    total, far_copies = sum_rows(1, near_copies)
    cosines, sines = angles_of(total, entries.at[1])
    for k in range(STEPS):
        last_turns[core, k : k + 1] = cosines[k]
        last_turns[core, STEPS + k : STEPS + k + 1] = sines[k]
    remote(last_turns.at[core], last_turns.at[core], turn_out.at[2], turn_in.at[2], other).start()
    angles_here = wait_all(last_turns.at[1 - core], turn_out.at[2], turn_in.at[2])
    far_copies.wait_send()
    angles_here.wait_recv()
    for pair in range(2):
        lines = [last_turns[pair, k : k + 1] for k in range(2 * STEPS)]
        left, right = turned(sides[pair, 0], sides[pair, 1], lines)
        o_ref[:, 2 * pair * BLK : (2 * pair + 1) * BLK] = left
        o_ref[:, (2 * pair + 1) * BLK : (2 * pair + 2) * BLK] = right

    angles_here.wait_send()


def on_device(n_rows, n_pairs, matrix, plan):
    rows, cols = matrix.shape
    dma = pltpu.SemaphoreType.DMA
    return pl.pallas_call(
        functools.partial(kernel, n_rows, n_pairs),
        out_shape=pltpu.VMEM((rows, cols), F32),
        in_specs=[
            pl.BlockSpec(memory_space=pl.ANY),
            pl.BlockSpec(memory_space=pl.ANY),
        ],
        out_specs=pl.BlockSpec(memory_space=pltpu.VMEM),
        scratch_shapes=[
            pltpu.VMEM((SLOTS, rows, BLK), F32),
            pltpu.VMEM((SLOTS, rows, BLK), F32),
            pltpu.VMEM((2, rows, BLK), F32),
            pltpu.VMEM((2, rows, BLK), F32),
            pltpu.VMEM((2, rows, BLK), F32),
            pltpu.VMEM((2, 2, rows, BLK), F32),
            pltpu.VMEM((2, 2, rows, BLK), F32),
            pltpu.VMEM((2, 2, rows, BLK), F32),
            pltpu.VMEM((ROUNDS, 2, ENTRIES, BLK), F32),
            pltpu.VMEM((ROUNDS, 2 * GROUP, ENTRIES, BLK), F32),
            pltpu.VMEM((ROUNDS, n_rows // 2 // GROUP, ENTRIES, BLK), F32),
            pltpu.VMEM((2, 4, 8, BLK), F32),
            pltpu.VMEM((2, 2 * STEPS, BLK), F32),
            pltpu.VMEM((2, 2, 2 * STEPS, BLK), F32),
            pltpu.VMEM((2, 2 * STEPS, BLK), F32),
            pltpu.SMEM((ROUNDS, n_pairs * SLOTS), jnp.int32),
            dma(()),
            pltpu.SemaphoreType.REGULAR((3,)),
            dma((SLOTS,)),
            dma((2,)),
            dma((2,)),
            dma((2,)),
            dma((2,)),
            dma((ROUNDS,)),
            dma((ROUNDS,)),
            dma((ROUNDS,)),
            dma((ROUNDS,)),
            dma((2,)),
            dma((2,)),
            dma((3,)),
            dma((3,)),
        ],
        compiler_params=pltpu.CompilerParams(
            collective_id=0, has_side_effects=True, vmem_limit_bytes=60 * 1024 * 1024
        ),
    )(plan, matrix)


def solution(mesh):
    return jax.shard_map(
        functools.partial(on_device, mesh.shape["rows"], mesh.shape["pairs"]),
        mesh=mesh,
        in_specs=(P("rows", "pairs"), P()),
        out_specs=P("rows", "pairs"),
        check_vma=False,
    )
```

```python
import functools

import jax
import jax.numpy as jnp
from jax import lax
from jax.experimental import pallas as pl
from jax.experimental.pallas import tpu as pltpu
from jax.sharding import PartitionSpec as P

MESH = pl.DeviceIdType.MESH
BLK = 128
ROUNDS = 2
STEPS = 4
SLOTS = 4
GROUP = 4
LANES = 128
ENTRIES = 16
F32 = jnp.float32
HOPS = ((3, 0), (3, 1), (2, 0), (2, 1), (1, 0), (1, 1), (0, 1))


def roll(x, by):
    return pltpu.roll(x, by % x.shape[1], 1)


def lane_of(shape):
    return lax.broadcasted_iota(jnp.int32, shape, 1)


def pick(x, index):
    return jnp.take_along_axis(x, index, axis=1)


def extra_lanes(slot):
    first = jnp.where(slot < 3, 0, jnp.where(slot < 5, 1, 2))
    second = jnp.where(slot < 3, 2 * slot + 1, jnp.where(slot == 3, 2, jnp.where(slot == 4, 4, 3)))
    return first, jnp.minimum(second, 7)


def band_terms(left, right, reverse):
    lane = lane_of(left.shape)
    top, bottom = left, pick(right, reverse)
    back = pick(left, reverse)
    tops = [top] + [roll(jnp.where(lane < d, right, top), -d) for d in (2, 4, 6)]
    bottoms = [bottom] + [roll(jnp.where(lane < d, back, bottom), -d) for d in (2, 4, 6)]
    first, second = extra_lanes(lane % 8)
    one = jnp.where(lane < 16, pick(top, first), pick(bottom, first))
    two = jnp.where(lane % 16 < 8, pick(top, second), pick(bottom, second))
    terms = [top * t for t in tops] + [top * b for b in bottoms]
    terms += [one * two] + [bottom * t for t in tops[1:]] + [bottom * b for b in bottoms]
    return top, bottom, terms


def fold(x):
    total = x[0:8]
    for first in range(8, x.shape[0], 8):
        total = total + x[first : first + 8]
    return total


def tangent_of(upper_a, lower_b, coupling):
    differ = lower_b - upper_a
    sign_val = jnp.where(differ >= 0.0, 1.0, -1.0)
    denom = jnp.abs(differ) + jnp.sqrt(differ * differ + 4.0 * coupling * coupling)
    positive = denom > 0.0
    safe_den = jnp.where(positive, denom, 1.0)
    return jnp.where(positive, 2.0 * coupling * sign_val / safe_den, 0.0)


def rotate_both(top, bottom, cosine, sine):
    return top * cosine - bottom * sine, top * sine + bottom * cosine


def angles(tt, tb, bt, bb):
    shape = tt.shape
    lane = lane_of(shape)
    row = lax.broadcasted_iota(jnp.int32, shape, 0)
    first, second = extra_lanes(jnp.minimum(lane, 5))
    ahead = lane + 2 * row
    over = ahead > LANES - 1
    is_extra = row == 4
    at_i = jnp.where(is_extra, first, lane)
    at_j = jnp.where(is_extra, second, jnp.where(row > 4, lane, jnp.where(over, 2 * LANES - 1 - ahead, ahead)))
    flip = jnp.where(over & (row < 4), -1.0, 1.0)

    def line(x, r):
        return jnp.broadcast_to(x[r : r + 1], shape)

    def item(x, r, i):
        return jnp.broadcast_to(x[r : r + 1, i : i + 1], shape)

    def up(x):
        return pltpu.roll(x, shape[0] - 1, 0)

    def down(x):
        return pltpu.roll(x, 1, 0)

    cosines, sines = [], []
    for step_no in range(STEPS):
        tangent = tangent_of(line(tt, 0), line(bb, 0), line(tb, 0))
        cosine = 1.0 / jnp.sqrt(1.0 + tangent * tangent)
        sine = cosine * tangent
        cosines.append(cosine[0:1])
        sines.append(sine[0:1])
        if step_no == STEPS - 1:
            break
        cos_i, sin_i = pick(cosine, at_i), pick(sine, at_i)
        cos_j, sin_j = pick(cosine, at_j), pick(sine, at_j) * flip
        tt, tb = rotate_both(tt, tb, cos_j, sin_j)
        bt, bb = rotate_both(bt, bb, cos_j, sin_j)
        tt, bt = rotate_both(tt, bt, cos_i, sin_i)
        tb, bb = rotate_both(tb, bb, cos_i, sin_i)
        new_tt = jnp.where(
            lane >= 2,
            roll(tt, 1),
            jnp.where(
                lane == 1,
                jnp.where(row == 0, roll(bb, 1), roll(bt, 1)),
                jnp.where(row == 0, tt, pick(line(tt, 4), jnp.maximum(row - 1, 0))),
            ),
        )
        new_bb = jnp.where(lane < LANES - 1, roll(bb, -1), pick(tt, LANES - 1 - 2 * row))
        new_tb = jnp.where(
            lane >= 2,
            roll(up(tb), 1),
            jnp.where(lane == 1, roll(up(bb), 1), pick(line(tb, 4), row)),
        )
        new_bt = jnp.where(
            row == 0,
            new_tb,
            jnp.where(
                lane < LANES - 1,
                roll(down(bt), -1),
                pick(down(bt), jnp.minimum(LANES + 1 - 2 * row, LANES - 1)),
            ),
        )
        head = lane == 0
        second_one = lane == 1
        extra_tt = jnp.where(head, item(tb, 0, 0), jnp.where(second_one, item(tt, 1, 0), item(bt, 4, 0)))
        extra_tb = jnp.where(head, item(tb, 1, 0), jnp.where(second_one, item(tb, 2, 0), item(bb, 4, 1)))
        extra_bt = jnp.where(head, item(bb, 4, 0), jnp.where(second_one, item(bt, 4, 3), item(tb, 4, 3)))
        extra_bb = jnp.where(head, item(bb, 4, 3), jnp.where(second_one, item(bb, 4, 4), item(bb, 4, 5)))
        tt = jnp.where(is_extra, extra_tt, new_tt)
        tb = jnp.where(is_extra, extra_tb, new_tb)
        bt = jnp.where(is_extra, extra_bt, new_bt)
        bb = jnp.where(is_extra, extra_bb, new_bb)
    return cosines, sines


def apply_steps(top, bottom, cosines, sines):
    lane = lane_of(top.shape)
    for step_no in range(STEPS):
        top, bottom = rotate_both(top, bottom, cosines[step_no], sines[step_no])
        if step_no < STEPS - 1:
            new_top = jnp.where(lane == 0, top, roll(jnp.where(lane == 0, bottom, top), 1))
            bottom = jnp.where(lane == LANES - 1, top, roll(bottom, -1))
            top = new_top
    last = STEPS - 1
    turn = 2 * LANES - 1 - last
    keep = LANES - last
    left = jnp.where(
        lane == 0,
        top,
        jnp.where(lane < keep, roll(top, -last), pick(bottom, jnp.minimum(turn - lane, LANES - 1))),
    )
    right = jnp.where(
        lane < keep, pick(bottom, jnp.maximum(turn - LANES - lane, 0)), roll(top, LANES - 1 - last)
    )
    return left, right


def kernel(
    n_rows, n_pairs, plan_in, x_ref, o_ref,
    first, second, third, came, sent, cross, crossed, sides, bands, parts, sums, entries, turns, far_turns, last_turns,
    plan_ref, plan_sem, ready_sem, in_sem, block_out, block_in, cross_out, cross_in, part_out, part_in,
    sum_out, sum_in, far_turn_out, far_turn_in, turn_out, turn_in,
):
    rows_at = lax.axis_index("rows")
    index = lax.axis_index("pairs")
    z, core = rows_at // 2, rows_at % 2
    n_chips = n_rows // 2
    group, member = z // GROUP, z % GROUP
    local_rows = x_ref.shape[0]

    def device(chip, which_core):
        return (chip * 2 + which_core, index)

    partner = [
        group * GROUP + at
        for at in (member, member + 1 - 2 * (member % 2), (member + 2) % GROUP, GROUP - 1 - member)
    ]
    near = [(which * 2 + turn, (core + turn) % 2, device(partner[which], (core + turn) % 2)) for which, turn in HOPS]
    near_slot = [
        ((member // 2 + at // 2) % 2 * 2 + (member + at) % 2) * 2 + (core + which_core) % 2
        for at in range(GROUP)
        for which_core in range(2)
    ]
    ahead = (rows_at, (index + 1) % n_pairs)
    behind = (rows_at, (index + n_pairs - 1) % n_pairs)
    across = jnp.where(member < 2, z + n_chips // 2 + 2, z + n_chips // 2 - 2) % n_chips
    n_groups = n_chips // GROUP
    far = [(2, device(across, core)), (3, device((z + GROUP) % n_chips, core)), (1, device((z + n_chips - GROUP) % n_chips, core))]
    far_slot = [(at + n_groups - group) % n_groups for at in range(n_groups)]
    has = (index < n_pairs - 1, index > 0)
    sides_here = has[::-1]
    line = [device((z + step + n_chips) % n_chips, core) for step in (1, -1, 2, -2)]
    other = device(z, 1 - core)
    peers = line[:2] + [other]
    barrier = pltpu.get_barrier_semaphore()
    for peer in peers:
        pl.semaphore_signal(barrier, inc=1, device_id=peer, device_id_type=MESH)
    for there, peer in zip(has, (ahead, behind)):

        @pl.when(there)
        def greet(peer=peer):
            pl.semaphore_signal(barrier, inc=1, device_id=peer, device_id_type=MESH)

    loads = [pltpu.make_async_copy(plan_in, plan_ref, plan_sem)] + [
        pltpu.make_async_copy(
            x_ref.at[:, pl.ds(s * BLK, BLK)], first.at[s], in_sem.at[s]
        )
        for s in range(SLOTS)
    ]
    for load in loads:
        load.start()
    for load in loads:
        load.wait()

    def remote(src, dst, send_sem, recv_sem, to):
        return pltpu.make_async_remote_copy(
            src_ref=src, dst_ref=dst, send_sem=send_sem, recv_sem=recv_sem,
            device_id=to, device_id_type=MESH,
        )

    shape = (8, LANES)
    reverse = LANES - 1 - lane_of((local_rows, LANES))
    pl.semaphore_wait(barrier, len(peers) + 2 - (index == 0) - (index == n_pairs - 1))

    def here(level, to):
        for peer in to:
            pl.semaphore_signal(ready_sem.at[level], inc=1, device_id=peer, device_id_type=MESH)

    def known(level):
        pl.semaphore_wait(ready_sem.at[level], 2)

    here(0, line[:2])

    def slots_taken(rnd, at):
        taken = jnp.int32(0)
        for s in range(SLOTS):
            took = plan_ref[rnd, at * SLOTS + s] - index * SLOTS
            taken = jnp.where((took >= 0) & (took < SLOTS), took, taken)
        return taken

    def band_sums(rnd, held, came):
        for pair in range(2):
            blocks = []
            for side in range(2):
                took = plan_ref[rnd, index * SLOTS + 2 * pair + side] - index * SLOTS
                own = held[jnp.clip(took, 0, SLOTS - 1)]
                blocks.append(jnp.where(took < 0, came[0], jnp.where(took >= SLOTS, came[1], own)))
            top, bottom, terms = band_terms(*blocks, reverse)
            sides[pair, 0] = top
            sides[pair, 1] = bottom
            for k in range(16):
                bands[rnd, pair, k : k + 1] = jnp.sum(fold(terms[k]), axis=0, keepdims=True)

    def wait_all(refs, send_sem, recv_sem):
        return remote(refs, refs, send_sem, recv_sem, other)

    def send_near(rnd):
        for slot, there, to in near:
            remote(
                bands.at[rnd, there], parts.at[rnd, slot], part_out.at[rnd], part_in.at[rnd], to
            ).start()
        parts[rnd, 0] = bands[rnd, core]
        return wait_all(parts.at[rnd, pl.ds(1, len(near))], part_out.at[rnd], part_in.at[rnd])

    def sum_rows(rnd, near_copies):
        near_copies.wait_recv()
        sums[rnd, 0] = in_order(parts.at[rnd], near_slot)
        if rnd == 0:
            known(2)
        for slot, to in far:
            remote(sums.at[rnd, 0], sums.at[rnd, slot], sum_out.at[rnd], sum_in.at[rnd], to).start()
        copies = wait_all(sums.at[rnd, pl.ds(1, len(far))], sum_out.at[rnd], sum_in.at[rnd])
        near_copies.wait_send()
        copies.wait_recv()
        total = in_order(sums.at[rnd], far_slot)
        return total, copies

    def in_order(ref, slots):
        total = ref[slots[0]]
        for slot in slots[1:]:
            total = total + ref[slot]
        return total

    def angles_of(total, work):
        work[...] = jnp.zeros(work.shape, F32)
        for k in range(4):
            work[k, 0:4] = total[4 * k : 4 * k + 4]
        work[2, 0:1] = total[4:5]
        for k in range(4):
            work[k, 4:5] = roll(jnp.broadcast_to(total[8:9], shape), -8 * k)[0:1]
        return angles(work[0], work[1], work[2], work[3])

    def spread(x):
        return jnp.broadcast_to(x, (local_rows, LANES))

    def turned(top, bottom, lines):
        wide = [spread(line) for line in lines]
        return apply_steps(top, bottom, wide[:STEPS], wide[STEPS:])

    def exchange(pairs_of_refs, send_sem, recv_sem):
        for way, to in enumerate((ahead, behind)):

            @pl.when(has[way])
            def start(way=way, to=to):
                for src, dst, which_core in pairs_of_refs(way):
                    device_to = (z * 2 + which_core, to[1])
                    remote(src, dst, send_sem.at[way], recv_sem.at[way], device_to).start()

        def wait(ref, received):
            for way in range(2):

                @pl.when(sides_here[way] if received else has[way])
                def one(way=way):
                    copy = wait_all(ref.at[way], send_sem.at[way], recv_sem.at[way])
                    if received:
                        copy.wait_recv()
                    else:
                        copy.wait_send()

        return wait

    for way, to in enumerate((ahead, behind)):
        sent[way] = first[slots_taken(0, to[1])]
    blocks = exchange(lambda way: [(sent.at[way], came.at[way], core)], block_out, block_in)
    known(0)
    here(1, line[2:])
    known(1)
    here(2, line[2:])
    blocks(came, True)
    band_sums(0, first, came)
    near_copies = send_near(0)

    for way, to in enumerate((ahead, behind)):
        from_second = slots_taken(1, to[1]) >= 2
        for side in range(2):
            cross[way, side] = jnp.where(from_second, sides[1, side], sides[0, side])
    columns = exchange(lambda way: [(cross.at[way], crossed.at[way], core)], cross_out, cross_in)
    blocks(came, False)

    total, far_copies = sum_rows(0, near_copies)
    cosines, sines = angles_of(total, entries.at[0])
    for k in range(STEPS):
        turns[core, k : k + 1] = cosines[k]
        turns[core, STEPS + k : STEPS + k + 1] = sines[k]
    far_angles = exchange(
        lambda way: [(turns.at[core], far_turns.at[way, core], which) for which in (core, 1 - core)],
        far_turn_out, far_turn_in,
    )
    remote(turns.at[core], turns.at[core], turn_out.at[1], turn_in.at[1], other).start()
    angles_here = wait_all(turns.at[1 - core], turn_out.at[1], turn_in.at[1])
    far_copies.wait_send()
    columns(crossed, False)
    angles_here.wait_recv()
    for pair in range(2):
        lines = [turns[pair, k : k + 1] for k in range(2 * STEPS)]
        left, right = turned(sides[pair, 0], sides[pair, 1], lines)
        second[2 * pair] = left
        second[2 * pair + 1] = right
    columns(crossed, True)
    far_angles(far_turns, True)
    for way in range(2):
        took = jnp.int32(0)
        for s in range(SLOTS):
            at = plan_ref[1, index * SLOTS + s] - index * SLOTS + (SLOTS, -SLOTS)[way]
            took = jnp.where((at >= 0) & (at < SLOTS), at, took)
        lines = [
            jnp.where(took >= 2, far_turns[way, 1, k : k + 1], far_turns[way, 0, k : k + 1])
            for k in range(2 * STEPS)
        ]
        left, right = turned(crossed[way, 0], crossed[way, 1], lines)
        third[way] = jnp.where((took == 1) | (took == 3), right, left)

    def place(pair, left, right):
        o_ref[:, pl.ds(pl.multiple_of(2 * pair * BLK, BLK), BLK)] = left
        o_ref[:, pl.ds(pl.multiple_of((2 * pair + 1) * BLK, BLK), BLK)] = right

    band_sums(1, second, third)
    near_copies = send_near(1)
    far_angles(far_turns, False)
    angles_here.wait_send()
    total, far_copies = sum_rows(1, near_copies)
    cosines, sines = angles_of(total, entries.at[1])
    for k in range(STEPS):
        last_turns[core, k : k + 1] = cosines[k]
        last_turns[core, STEPS + k : STEPS + k + 1] = sines[k]
    remote(last_turns.at[core], last_turns.at[core], turn_out.at[2], turn_in.at[2], other).start()
    angles_here = wait_all(last_turns.at[1 - core], turn_out.at[2], turn_in.at[2])
    far_copies.wait_send()
    left, right = turned(sides[core, 0], sides[core, 1], cosines + sines)
    place(core, left, right)
    angles_here.wait_recv()
    lines = [last_turns[1 - core, k : k + 1] for k in range(2 * STEPS)]
    left, right = turned(sides[1 - core, 0], sides[1 - core, 1], lines)
    place(1 - core, left, right)
    angles_here.wait_send()


def on_device(n_rows, n_pairs, matrix, plan):
    rows, cols = matrix.shape
    dma = pltpu.SemaphoreType.DMA
    return pl.pallas_call(
        functools.partial(kernel, n_rows, n_pairs),
        out_shape=pltpu.VMEM((rows, cols), F32),
        in_specs=[
            pl.BlockSpec(memory_space=pl.ANY),
            pl.BlockSpec(memory_space=pl.ANY),
        ],
        out_specs=pl.BlockSpec(memory_space=pltpu.VMEM),
        scratch_shapes=[
            pltpu.VMEM((SLOTS, rows, BLK), F32),
            pltpu.VMEM((SLOTS, rows, BLK), F32),
            pltpu.VMEM((2, rows, BLK), F32),
            pltpu.VMEM((2, rows, BLK), F32),
            pltpu.VMEM((2, rows, BLK), F32),
            pltpu.VMEM((2, 2, rows, BLK), F32),
            pltpu.VMEM((2, 2, rows, BLK), F32),
            pltpu.VMEM((2, 2, rows, BLK), F32),
            pltpu.VMEM((ROUNDS, 2, ENTRIES, BLK), F32),
            pltpu.VMEM((ROUNDS, 2 * GROUP, ENTRIES, BLK), F32),
            pltpu.VMEM((ROUNDS, n_rows // 2 // GROUP, ENTRIES, BLK), F32),
            pltpu.VMEM((2, 4, 8, BLK), F32),
            pltpu.VMEM((2, 2 * STEPS, BLK), F32),
            pltpu.VMEM((2, 2, 2 * STEPS, BLK), F32),
            pltpu.VMEM((2, 2 * STEPS, BLK), F32),
            pltpu.SMEM((ROUNDS, n_pairs * SLOTS), jnp.int32),
            dma(()),
            pltpu.SemaphoreType.REGULAR((3,)),
            dma((SLOTS,)),
            dma((2,)),
            dma((2,)),
            dma((2,)),
            dma((2,)),
            dma((ROUNDS,)),
            dma((ROUNDS,)),
            dma((ROUNDS,)),
            dma((ROUNDS,)),
            dma((2,)),
            dma((2,)),
            dma((3,)),
            dma((3,)),
        ],
        compiler_params=pltpu.CompilerParams(
            collective_id=0, has_side_effects=True, vmem_limit_bytes=60 * 1024 * 1024
        ),
    )(plan, matrix)


def solution(mesh):
    return jax.shard_map(
        functools.partial(on_device, mesh.shape["rows"], mesh.shape["pairs"]),
        mesh=mesh,
        in_specs=(P("rows", "pairs"), P()),
        out_specs=P("rows", "pairs"),
        check_vma=False,
    )
```

```python
import functools

import jax
import jax.numpy as jnp
from jax import lax
from jax.experimental import pallas as pl
from jax.experimental.pallas import tpu as pltpu
from jax.sharding import PartitionSpec as P

MESH = pl.DeviceIdType.MESH
BLK = 128
ROUNDS = 2
STEPS = 4
SLOTS = 4
GROUP = 4
LANES = 128
ENTRIES = 16
F32 = jnp.float32
HOPS = ((3, 0), (3, 1), (2, 0), (2, 1), (1, 0), (1, 1), (0, 1))


def roll(x, by):
    return pltpu.roll(x, by % x.shape[1], 1)


def lane_of(shape):
    return lax.broadcasted_iota(jnp.int32, shape, 1)


def pick(x, index):
    return jnp.take_along_axis(x, index, axis=1)


def extra_lanes(slot):
    first = jnp.where(slot < 3, 0, jnp.where(slot < 5, 1, 2))
    second = jnp.where(slot < 3, 2 * slot + 1, jnp.where(slot == 3, 2, jnp.where(slot == 4, 4, 3)))
    return first, jnp.minimum(second, 7)


def band_terms(left, right, reverse):
    lane = lane_of(left.shape)
    top, bottom = left, pick(right, reverse)
    back = pick(left, reverse)
    tops = [top] + [roll(jnp.where(lane < d, right, top), -d) for d in (2, 4, 6)]
    bottoms = [bottom] + [roll(jnp.where(lane < d, back, bottom), -d) for d in (2, 4, 6)]
    first, second = extra_lanes(lane % 8)
    one = jnp.where(lane < 16, pick(top, first), pick(bottom, first))
    two = jnp.where(lane % 16 < 8, pick(top, second), pick(bottom, second))
    terms = [top * t for t in tops] + [top * b for b in bottoms]
    terms += [one * two] + [bottom * t for t in tops[1:]] + [bottom * b for b in bottoms]
    return top, bottom, terms


def fold(x):
    total = x[0:8]
    for first in range(8, x.shape[0], 8):
        total = total + x[first : first + 8]
    return total


def tangent_of(upper_a, lower_b, coupling):
    differ = lower_b - upper_a
    sign_val = jnp.where(differ >= 0.0, 1.0, -1.0)
    denom = jnp.abs(differ) + jnp.sqrt(differ * differ + 4.0 * coupling * coupling)
    positive = denom > 0.0
    safe_den = jnp.where(positive, denom, 1.0)
    return jnp.where(positive, 2.0 * coupling * sign_val / safe_den, 0.0)


def rotate_both(top, bottom, cosine, sine):
    return top * cosine - bottom * sine, top * sine + bottom * cosine


def angles(tt, tb, bt, bb):
    shape = tt.shape
    lane = lane_of(shape)
    row = lax.broadcasted_iota(jnp.int32, shape, 0)
    first, second = extra_lanes(jnp.minimum(lane, 5))
    ahead = lane + 2 * row
    over = ahead > LANES - 1
    is_extra = row == 4
    at_i = jnp.where(is_extra, first, lane)
    at_j = jnp.where(is_extra, second, jnp.where(row > 4, lane, jnp.where(over, 2 * LANES - 1 - ahead, ahead)))
    flip = jnp.where(over & (row < 4), -1.0, 1.0)

    def line(x, r):
        return jnp.broadcast_to(x[r : r + 1], shape)

    def item(x, r, i):
        return jnp.broadcast_to(x[r : r + 1, i : i + 1], shape)

    def up(x):
        return pltpu.roll(x, shape[0] - 1, 0)

    def down(x):
        return pltpu.roll(x, 1, 0)

    cosines, sines = [], []
    for step_no in range(STEPS):
        tangent = tangent_of(line(tt, 0), line(bb, 0), line(tb, 0))
        cosine = 1.0 / jnp.sqrt(1.0 + tangent * tangent)
        sine = cosine * tangent
        cosines.append(cosine[0:1])
        sines.append(sine[0:1])
        if step_no == STEPS - 1:
            break
        cos_i, sin_i = pick(cosine, at_i), pick(sine, at_i)
        cos_j, sin_j = pick(cosine, at_j), pick(sine, at_j) * flip
        tt, tb = rotate_both(tt, tb, cos_j, sin_j)
        bt, bb = rotate_both(bt, bb, cos_j, sin_j)
        tt, bt = rotate_both(tt, bt, cos_i, sin_i)
        tb, bb = rotate_both(tb, bb, cos_i, sin_i)
        new_tt = jnp.where(
            lane >= 2,
            roll(tt, 1),
            jnp.where(
                lane == 1,
                jnp.where(row == 0, roll(bb, 1), roll(bt, 1)),
                jnp.where(row == 0, tt, pick(line(tt, 4), jnp.maximum(row - 1, 0))),
            ),
        )
        new_bb = jnp.where(lane < LANES - 1, roll(bb, -1), pick(tt, LANES - 1 - 2 * row))
        new_tb = jnp.where(
            lane >= 2,
            roll(up(tb), 1),
            jnp.where(lane == 1, roll(up(bb), 1), pick(line(tb, 4), row)),
        )
        new_bt = jnp.where(
            row == 0,
            new_tb,
            jnp.where(
                lane < LANES - 1,
                roll(down(bt), -1),
                pick(down(bt), jnp.minimum(LANES + 1 - 2 * row, LANES - 1)),
            ),
        )
        head = lane == 0
        second_one = lane == 1
        extra_tt = jnp.where(head, item(tb, 0, 0), jnp.where(second_one, item(tt, 1, 0), item(bt, 4, 0)))
        extra_tb = jnp.where(head, item(tb, 1, 0), jnp.where(second_one, item(tb, 2, 0), item(bb, 4, 1)))
        extra_bt = jnp.where(head, item(bb, 4, 0), jnp.where(second_one, item(bt, 4, 3), item(tb, 4, 3)))
        extra_bb = jnp.where(head, item(bb, 4, 3), jnp.where(second_one, item(bb, 4, 4), item(bb, 4, 5)))
        tt = jnp.where(is_extra, extra_tt, new_tt)
        tb = jnp.where(is_extra, extra_tb, new_tb)
        bt = jnp.where(is_extra, extra_bt, new_bt)
        bb = jnp.where(is_extra, extra_bb, new_bb)
    return cosines, sines


def apply_steps(top, bottom, cosines, sines):
    lane = lane_of(top.shape)
    for step_no in range(STEPS):
        top, bottom = rotate_both(top, bottom, cosines[step_no], sines[step_no])
        if step_no < STEPS - 1:
            new_top = jnp.where(lane == 0, top, roll(jnp.where(lane == 0, bottom, top), 1))
            bottom = jnp.where(lane == LANES - 1, top, roll(bottom, -1))
            top = new_top
    last = STEPS - 1
    turn = 2 * LANES - 1 - last
    keep = LANES - last
    left = jnp.where(
        lane == 0,
        top,
        jnp.where(lane < keep, roll(top, -last), pick(bottom, jnp.minimum(turn - lane, LANES - 1))),
    )
    right = jnp.where(
        lane < keep, pick(bottom, jnp.maximum(turn - LANES - lane, 0)), roll(top, LANES - 1 - last)
    )
    return left, right


def kernel(
    n_rows, n_pairs, plan_in, x_ref, o_ref,
    first, second, third, came, sent, cross, crossed, sides, bands, parts, sums, entries, turns, far_turns, last_turns,
    plan_ref, plan_sem, ready_sem, in_sem, block_out, block_in, cross_out, cross_in, part_out, part_in,
    sum_out, sum_in, far_turn_out, far_turn_in, turn_out, turn_in,
):
    rows_at = lax.axis_index("rows")
    index = lax.axis_index("pairs")
    z, core = rows_at // 2, rows_at % 2
    n_chips = n_rows // 2
    group, member = z // GROUP, z % GROUP
    local_rows = x_ref.shape[0]

    def device(chip, which_core):
        return (chip * 2 + which_core, index)

    partner = [
        group * GROUP + at
        for at in (member, member + 1 - 2 * (member % 2), (member + 2) % GROUP, GROUP - 1 - member)
    ]
    near = [(which * 2 + turn, (core + turn) % 2, device(partner[which], (core + turn) % 2)) for which, turn in HOPS]
    near_slot = [
        ((member // 2 + at // 2) % 2 * 2 + (member + at) % 2) * 2 + (core + which_core) % 2
        for at in range(GROUP)
        for which_core in range(2)
    ]
    ahead = (rows_at, (index + 1) % n_pairs)
    behind = (rows_at, (index + n_pairs - 1) % n_pairs)
    across = jnp.where(member < 2, z + n_chips // 2 + 2, z + n_chips // 2 - 2) % n_chips
    n_groups = n_chips // GROUP
    far = [(2, device(across, core)), (3, device((z + GROUP) % n_chips, core)), (1, device((z + n_chips - GROUP) % n_chips, core))]
    far_slot = [(at + n_groups - group) % n_groups for at in range(n_groups)]
    has = (index < n_pairs - 1, index > 0)
    sides_here = has[::-1]
    line = [device((z + step + n_chips) % n_chips, core) for step in (1, -1, 2, -2)]
    other = device(z, 1 - core)
    peers = line[:2] + [other]
    barrier = pltpu.get_barrier_semaphore()
    for peer in peers:
        pl.semaphore_signal(barrier, inc=1, device_id=peer, device_id_type=MESH)
    for there, peer in zip(has, (ahead, behind)):

        @pl.when(there)
        def greet(peer=peer):
            pl.semaphore_signal(barrier, inc=1, device_id=peer, device_id_type=MESH)

    loads = [pltpu.make_async_copy(plan_in, plan_ref, plan_sem)] + [
        pltpu.make_async_copy(
            x_ref.at[:, pl.ds(s * BLK, BLK)], first.at[s], in_sem.at[s]
        )
        for s in range(SLOTS)
    ]
    for load in loads:
        load.start()
    for load in loads:
        load.wait()

    def remote(src, dst, send_sem, recv_sem, to):
        return pltpu.make_async_remote_copy(
            src_ref=src, dst_ref=dst, send_sem=send_sem, recv_sem=recv_sem,
            device_id=to, device_id_type=MESH,
        )

    shape = (8, LANES)
    reverse = LANES - 1 - lane_of((local_rows, LANES))
    pl.semaphore_wait(barrier, len(peers) + 2 - (index == 0) - (index == n_pairs - 1))

    def here(level, to):
        for peer in to:
            pl.semaphore_signal(ready_sem.at[level], inc=1, device_id=peer, device_id_type=MESH)

    def known(level):
        pl.semaphore_wait(ready_sem.at[level], 2)

    here(0, line[:2])

    def slots_taken(rnd, at):
        taken = jnp.int32(0)
        for s in range(SLOTS):
            took = plan_ref[rnd, at * SLOTS + s] - index * SLOTS
            taken = jnp.where((took >= 0) & (took < SLOTS), took, taken)
        return taken

    def band_sums(rnd, held, came):
        for pair in range(2):
            blocks = []
            for side in range(2):
                took = plan_ref[rnd, index * SLOTS + 2 * pair + side] - index * SLOTS
                own = held[jnp.clip(took, 0, SLOTS - 1)]
                blocks.append(jnp.where(took < 0, came[0], jnp.where(took >= SLOTS, came[1], own)))
            top, bottom, terms = band_terms(*blocks, reverse)
            sides[pair, 0] = top
            sides[pair, 1] = bottom
            for k in range(16):
                bands[rnd, pair, k : k + 1] = jnp.sum(fold(terms[k]), axis=0, keepdims=True)
            for which in (3, 2, 1):
                remote(
                    bands.at[rnd, pair], parts.at[rnd, which * 2 + (core + pair) % 2],
                    part_out.at[rnd], part_in.at[rnd], device(partner[which], pair),
                ).start()

    def wait_all(refs, send_sem, recv_sem):
        return remote(refs, refs, send_sem, recv_sem, other)

    def send_near(rnd):
        slot, there, to = near[-1]
        remote(bands.at[rnd, there], parts.at[rnd, slot], part_out.at[rnd], part_in.at[rnd], to).start()
        parts[rnd, 0] = bands[rnd, core]
        return wait_all(parts.at[rnd, pl.ds(1, len(near))], part_out.at[rnd], part_in.at[rnd])

    def sum_rows(rnd, near_copies):
        near_copies.wait_recv()
        sums[rnd, 0] = in_order(parts.at[rnd], near_slot)
        if rnd == 0:
            known(2)
        for slot, to in far:
            remote(sums.at[rnd, 0], sums.at[rnd, slot], sum_out.at[rnd], sum_in.at[rnd], to).start()
        copies = wait_all(sums.at[rnd, pl.ds(1, len(far))], sum_out.at[rnd], sum_in.at[rnd])
        near_copies.wait_send()
        copies.wait_recv()
        total = in_order(sums.at[rnd], far_slot)
        return total, copies

    def in_order(ref, slots):
        total = ref[slots[0]]
        for slot in slots[1:]:
            total = total + ref[slot]
        return total

    def angles_of(total, work):
        work[...] = jnp.zeros(work.shape, F32)
        for k in range(4):
            work[k, 0:4] = total[4 * k : 4 * k + 4]
        work[2, 0:1] = total[4:5]
        for k in range(4):
            work[k, 4:5] = roll(jnp.broadcast_to(total[8:9], shape), -8 * k)[0:1]
        return angles(work[0], work[1], work[2], work[3])

    def spread(x):
        return jnp.broadcast_to(x, (local_rows, LANES))

    def turned(top, bottom, lines):
        wide = [spread(line) for line in lines]
        return apply_steps(top, bottom, wide[:STEPS], wide[STEPS:])

    def exchange(pairs_of_refs, send_sem, recv_sem):
        for way, to in enumerate((ahead, behind)):

            @pl.when(has[way])
            def start(way=way, to=to):
                for src, dst, which_core in pairs_of_refs(way):
                    device_to = (z * 2 + which_core, to[1])
                    remote(src, dst, send_sem.at[way], recv_sem.at[way], device_to).start()

        def wait(ref, received):
            for way in range(2):

                @pl.when(sides_here[way] if received else has[way])
                def one(way=way):
                    copy = wait_all(ref.at[way], send_sem.at[way], recv_sem.at[way])
                    if received:
                        copy.wait_recv()
                    else:
                        copy.wait_send()

        return wait

    for way, to in enumerate((ahead, behind)):
        sent[way] = first[slots_taken(0, to[1])]
    blocks = exchange(lambda way: [(sent.at[way], came.at[way], core)], block_out, block_in)
    known(0)
    here(1, line[2:])
    known(1)
    here(2, line[2:])
    blocks(came, True)
    band_sums(0, first, came)
    near_copies = send_near(0)

    for way, to in enumerate((ahead, behind)):
        from_second = slots_taken(1, to[1]) >= 2
        for side in range(2):
            cross[way, side] = jnp.where(from_second, sides[1, side], sides[0, side])
    columns = exchange(lambda way: [(cross.at[way], crossed.at[way], core)], cross_out, cross_in)
    blocks(came, False)

    total, far_copies = sum_rows(0, near_copies)
    cosines, sines = angles_of(total, entries.at[0])
    for k in range(STEPS):
        turns[core, k : k + 1] = cosines[k]
        turns[core, STEPS + k : STEPS + k + 1] = sines[k]
    far_angles = exchange(
        lambda way: [(turns.at[core], far_turns.at[way, core], which) for which in (core, 1 - core)],
        far_turn_out, far_turn_in,
    )
    remote(turns.at[core], turns.at[core], turn_out.at[1], turn_in.at[1], other).start()
    angles_here = wait_all(turns.at[1 - core], turn_out.at[1], turn_in.at[1])
    far_copies.wait_send()
    columns(crossed, False)
    angles_here.wait_recv()
    for pair in range(2):
        lines = [turns[pair, k : k + 1] for k in range(2 * STEPS)]
        left, right = turned(sides[pair, 0], sides[pair, 1], lines)
        second[2 * pair] = left
        second[2 * pair + 1] = right
    columns(crossed, True)
    far_angles(far_turns, True)
    for way in range(2):
        took = jnp.int32(0)
        for s in range(SLOTS):
            at = plan_ref[1, index * SLOTS + s] - index * SLOTS + (SLOTS, -SLOTS)[way]
            took = jnp.where((at >= 0) & (at < SLOTS), at, took)
        lines = [
            jnp.where(took >= 2, far_turns[way, 1, k : k + 1], far_turns[way, 0, k : k + 1])
            for k in range(2 * STEPS)
        ]
        left, right = turned(crossed[way, 0], crossed[way, 1], lines)
        third[way] = jnp.where((took == 1) | (took == 3), right, left)

    def place(pair, left, right):
        o_ref[:, pl.ds(pl.multiple_of(2 * pair * BLK, BLK), BLK)] = left
        o_ref[:, pl.ds(pl.multiple_of((2 * pair + 1) * BLK, BLK), BLK)] = right

    band_sums(1, second, third)
    near_copies = send_near(1)
    far_angles(far_turns, False)
    angles_here.wait_send()
    total, far_copies = sum_rows(1, near_copies)
    cosines, sines = angles_of(total, entries.at[1])
    for k in range(STEPS):
        last_turns[core, k : k + 1] = cosines[k]
        last_turns[core, STEPS + k : STEPS + k + 1] = sines[k]
    remote(last_turns.at[core], last_turns.at[core], turn_out.at[2], turn_in.at[2], other).start()
    angles_here = wait_all(last_turns.at[1 - core], turn_out.at[2], turn_in.at[2])
    far_copies.wait_send()
    left, right = turned(sides[core, 0], sides[core, 1], cosines + sines)
    place(core, left, right)
    angles_here.wait_recv()
    lines = [last_turns[1 - core, k : k + 1] for k in range(2 * STEPS)]
    left, right = turned(sides[1 - core, 0], sides[1 - core, 1], lines)
    place(1 - core, left, right)
    angles_here.wait_send()


def on_device(n_rows, n_pairs, matrix, plan):
    rows, cols = matrix.shape
    dma = pltpu.SemaphoreType.DMA
    return pl.pallas_call(
        functools.partial(kernel, n_rows, n_pairs),
        out_shape=pltpu.VMEM((rows, cols), F32),
        in_specs=[
            pl.BlockSpec(memory_space=pl.ANY),
            pl.BlockSpec(memory_space=pl.ANY),
        ],
        out_specs=pl.BlockSpec(memory_space=pltpu.VMEM),
        scratch_shapes=[
            pltpu.VMEM((SLOTS, rows, BLK), F32),
            pltpu.VMEM((SLOTS, rows, BLK), F32),
            pltpu.VMEM((2, rows, BLK), F32),
            pltpu.VMEM((2, rows, BLK), F32),
            pltpu.VMEM((2, rows, BLK), F32),
            pltpu.VMEM((2, 2, rows, BLK), F32),
            pltpu.VMEM((2, 2, rows, BLK), F32),
            pltpu.VMEM((2, 2, rows, BLK), F32),
            pltpu.VMEM((ROUNDS, 2, ENTRIES, BLK), F32),
            pltpu.VMEM((ROUNDS, 2 * GROUP, ENTRIES, BLK), F32),
            pltpu.VMEM((ROUNDS, n_rows // 2 // GROUP, ENTRIES, BLK), F32),
            pltpu.VMEM((2, 4, 8, BLK), F32),
            pltpu.VMEM((2, 2 * STEPS, BLK), F32),
            pltpu.VMEM((2, 2, 2 * STEPS, BLK), F32),
            pltpu.VMEM((2, 2 * STEPS, BLK), F32),
            pltpu.SMEM((ROUNDS, n_pairs * SLOTS), jnp.int32),
            dma(()),
            pltpu.SemaphoreType.REGULAR((3,)),
            dma((SLOTS,)),
            dma((2,)),
            dma((2,)),
            dma((2,)),
            dma((2,)),
            dma((ROUNDS,)),
            dma((ROUNDS,)),
            dma((ROUNDS,)),
            dma((ROUNDS,)),
            dma((2,)),
            dma((2,)),
            dma((3,)),
            dma((3,)),
        ],
        compiler_params=pltpu.CompilerParams(
            collective_id=0, has_side_effects=True, vmem_limit_bytes=60 * 1024 * 1024
        ),
    )(plan, matrix)


def solution(mesh):
    return jax.shard_map(
        functools.partial(on_device, mesh.shape["rows"], mesh.shape["pairs"]),
        mesh=mesh,
        in_specs=(P("rows", "pairs"), P()),
        out_specs=P("rows", "pairs"),
        check_vma=False,
    )
```
